256 devices in a mesh: ctx: 32 (over x, y, core), tp: 8 (over z).
Axes of the slice: x: 4, y: 4, z: 8, core: 2. Of those that a mesh axis runs over, the one named last changes fastest.
Arguments:
- queries: bfloat16 [8192, 7168], P('ctx', 'tp'), may hold values from -6 to 6
- new_kv: bfloat16 [2, 8192, 1024], P(None, 'ctx', 'tp'), may hold values from -6 to 6
- page_cache: bfloat16 [2, 8192, 1024], P(None, 'ctx', 'tp'), may hold values from -6 to 6
- out_weight: bfloat16 [7168, 7168], P('tp', 'ctx'), may hold values from -0.5 to 0.5
- page_slot: int32 [64], replicated, may hold values from 0 to 63, each once
- parent: int32 [64], replicated, may hold values from -1 to 62, as said below
- valid_count: int32 [64], replicated, may hold values from 1 to 128
- lost_parent: int32 [64], replicated, may hold values from 0 to 63
Outputs:
- mixed: bfloat16 [8192, 7168], P('ctx', 'tp')
The draws below stay inside these ranges and needn't reach their ends.
Inputs may be any that keep to these rules, and one draw needn't show every extreme that they name: parent[p] < p for p >= 1 and parent[0] = -1.
All inputs are finite; a program needn't handle non-finite values.
Results may differ from the reference program's by a relative error of at most 0.02.
Values may be sent and summed in bfloat16 or wider, within the bound.
A program may use at most 128 MiB of HBM per device.

```python
import math
import jax
import jax.numpy as jnp
from jax import lax

D = 7168
HEADS = 56
KV_HEADS = 8
HD = 128
PAGE = 128
LOST = 64
SURV = 64


def draw_queries(key, part):
    key = jax.random.fold_in(key, 11)
    drawn = jnp.clip(jax.random.normal(key, (LOST * PAGE, HEADS * HD), jnp.float32), -6.0, 6.0)
    return drawn.astype(jnp.bfloat16)


def draw_new_kv(key, part):
    key = jax.random.fold_in(key, 23)
    drawn = jnp.clip(jax.random.normal(key, (2, LOST * PAGE, KV_HEADS * HD), jnp.float32), -6.0, 6.0)
    return drawn.astype(jnp.bfloat16)


def draw_parent(key, part):
    key = jax.random.fold_in(key, 37)
    steps_back = jax.random.randint(key, (SURV,), 1, 4, dtype=jnp.int32)
    page_ids = jnp.arange(SURV, dtype=jnp.int32)
    steps_back = jnp.where(page_ids == SURV - 1, 1, steps_back)
    return jnp.where(page_ids == 0, -1, jnp.maximum(page_ids - steps_back, 0)).astype(jnp.int32)


def plant(values, rng, least, largest):
    longest = values.shape.index(max(values.shape))
    spots = []
    for shift in (0, 1):
        where = [jax.random.randint(jax.random.fold_in(rng, axis), (), 0, length) for axis, length in enumerate(values.shape)]
        where[longest] = (where[longest] + shift) % values.shape[longest]
        spots.append(tuple(where))
    return values.at[spots[0]].set(least).at[spots[1]].set(largest)


def shard_levels(stream_key, shape, cuts, low, top_value):
    gain = 1.0
    for axis_at, blocks in cuts:
        draws = jax.random.uniform(jax.random.fold_in(jax.random.fold_in(stream_key, 6), axis_at), (blocks,), jnp.float32, low / len(cuts), top_value / len(cuts))
        gain = gain * jnp.repeat(jnp.exp(draws), shape[axis_at] // blocks).reshape((-1,) + (1,) * (len(shape) - 1 - axis_at))
    return gain


def scatter_about(own_key, shape, spread, bound, cuts=(), kind=jnp.bfloat16):
    level = shard_levels(own_key, shape, cuts, -0.22, 0.18) if cuts else 1.0
    result = jax.random.normal(own_key, shape, jnp.float32) * spread * level
    return jnp.minimum(jnp.maximum(result, -bound), bound).astype(kind)


def setup_inputs(seed: int = 0) -> dict:
    key_of = jax.random.split(jax.random.key(seed), 9)
    return {
        "queries": draw_queries(jax.random.fold_in(key_of[8], 71), 0),
        "new_kv": draw_new_kv(jax.random.fold_in(key_of[8], 71), 0),
        "page_cache": scatter_about(key_of[2], (2, SURV * PAGE, KV_HEADS * HD), 1.0, 6.0, ((1, 32), (2, 8))),
        "out_weight": scatter_about(key_of[3], (HEADS * HD, D), HD ** -0.5, 0.5, ((0, 8), (1, 32))),
        "page_slot": jax.random.permutation(key_of[4], SURV).astype(jnp.int32),
        "parent": draw_parent(jax.random.fold_in(key_of[8], 71), 0),
        "valid_count": plant(jax.random.randint(key_of[6], (SURV,), 1, PAGE + 1), jax.random.fold_in(key_of[6], 1), 1, PAGE).astype(jnp.int32),
        "lost_parent": plant(jax.random.randint(key_of[7], (LOST,), 0, SURV), jax.random.fold_in(key_of[7], 1), 0, SURV - 1).astype(jnp.int32),
    }


def reference(queries, new_kv, page_cache, out_weight, page_slot, parent, valid_count, lost_parent):
    group_size = HEADS // KV_HEADS
    score_scale = 1.0 / math.sqrt(HD)
    page_ids = jnp.arange(SURV, dtype=jnp.int32)

    def climb(state, unused):
        current, onpath = state
        onpath = onpath | (current[:, None] == page_ids[None, :])
        climbed = jnp.where(current >= 0, parent[jnp.maximum(current, 0)], -1).astype(jnp.int32)
        return ((climbed, onpath), None)
    start_state = (lost_parent.astype(jnp.int32), jnp.zeros((LOST, SURV), bool))
    (unused_final, onpath), unused_out = lax.scan(climb, start_state, None, length=SURV)
    by_page = page_cache.reshape(2, SURV, PAGE, KV_HEADS * HD)[:, page_slot]
    keys_all = by_page[0].reshape(SURV * PAGE, KV_HEADS, HD).astype(jnp.float32)
    values_all = by_page[1].reshape(SURV * PAGE, KV_HEADS, HD).astype(jnp.float32)
    tokens = jnp.arange(PAGE, dtype=jnp.int32)
    kept_keys = onpath[:, :, None] & (tokens[None, None, :] < valid_count[None, :, None])
    causal = tokens[None, :] <= tokens[:, None]

    def one_page(lost_index):
        query_block = lax.dynamic_slice_in_dim(queries, lost_index * PAGE, PAGE, 0)
        query_block = query_block.astype(jnp.float32).reshape(PAGE, KV_HEADS, group_size, HD)
        fresh_kv = lax.dynamic_slice_in_dim(new_kv, lost_index * PAGE, PAGE, 1)
        fresh_kv = fresh_kv.astype(jnp.float32).reshape(2, PAGE, KV_HEADS, HD)
        key_rows = jnp.concatenate([keys_all, fresh_kv[0]], axis=0)
        value_rows = jnp.concatenate([values_all, fresh_kv[1]], axis=0)
        path_keys = jnp.broadcast_to(kept_keys[lost_index].reshape(1, SURV * PAGE), (PAGE, SURV * PAGE))
        visible = jnp.concatenate([path_keys, causal], axis=1)
        scores = jnp.einsum('qkgd,nkd->kgqn', query_block, key_rows) * score_scale
        scores = jnp.where(visible, scores, -1e+30)
        row_max = lax.optimization_barrier(jnp.max(scores, axis=-1, keepdims=True))
        weights = jnp.exp(scores - row_max) * visible.astype(jnp.float32)
        weight_sum = lax.optimization_barrier(jnp.sum(weights, axis=-1))
        rounded = lax.optimization_barrier(weights.astype(jnp.bfloat16)).astype(jnp.float32)
        mixed_heads = jnp.einsum('kgqn,nkd->kgqd', rounded, value_rows) / weight_sum[..., None]
        return jnp.transpose(mixed_heads, (2, 0, 1, 3)).reshape(PAGE, HEADS * HD).astype(jnp.bfloat16)
    attended = lax.map(one_page, jnp.arange(LOST, dtype=jnp.int32)).reshape(LOST * PAGE, HEADS * HD)
    return jnp.dot(attended, out_weight, preferred_element_type=jnp.float32).astype(jnp.bfloat16)
```

```python
import math

import jax
import jax.numpy as jnp
from jax import lax
from jax.experimental import pallas as pl
from jax.experimental.pallas import tpu as pltpu
from jax.sharding import PartitionSpec as P

HEADS = 56
KV_HEADS = 8
HD = 128
PAGE = 128
GROUP = HEADS // KV_HEADS
CHUNK = 512
MESH = pl.DeviceIdType.MESH
VMEM_LIMIT = 56 * 2**20


def place():
    c = lax.axis_index("ctx")
    return lax.div(c, 8), lax.rem(lax.div(c, 2), 4), lax.rem(c, 2), lax.axis_index("tp")


def ctx_of(x, y, k):
    return (x * 4 + y) * 2 + k


def gather_kernel(page_ref, kv_ref, own_sem, send1, recv1, send2, recv2, core_send, core_recv):
    x, y, k, t = place()

    def at_x(d):
        return (ctx_of(lax.rem(x + d, 4), y, k), t)

    def at_y(d):
        return (ctx_of(x, lax.rem(y + d, 4), k), t)

    other = (ctx_of(x, y, 1 - k), t)
    barrier = pltpu.get_barrier_semaphore()
    for d in (1, 2, 3):
        pl.semaphore_signal(barrier, inc=1, device_id=at_x(d), device_id_type=MESH)
        pl.semaphore_signal(barrier, inc=1, device_id=at_y(d), device_id_type=MESH)
    pl.semaphore_signal(barrier, inc=1, device_id=other, device_id_type=MESH)
    own = pltpu.make_async_copy(page_ref, kv_ref.at[:, x, y, k], own_sem)
    own.start()
    pl.semaphore_wait(barrier, 7)

    def remote(src, dst, send, recv, device):
        return pltpu.make_async_remote_copy(
            src, dst, send, recv, device_id=device, device_id_type=MESH
        )

    first = {}
    for d in (2, 1, 3):
        first[0, d] = remote(page_ref.at[0], kv_ref.at[0, x, y, k], send1.at[0, d], recv1.at[0, d], at_x(d))
        first[1, d] = remote(page_ref.at[1], kv_ref.at[1, x, y, k], send1.at[1, d], recv1.at[1, d], at_y(d))
        first[0, d].start()
        first[1, d].start()
    own.wait()
    for d in (1, 3, 2):
        first[0, d].wait_recv()
        first[1, d].wait_recv()
    row_block = kv_ref.at[0, :, y, k]
    column_block = kv_ref.at[1, x, :, k]
    second = {}
    for d in (2, 1, 3):
        second[0, d] = remote(row_block, row_block, send2.at[0, d], recv2.at[0, d], at_y(d))
        second[1, d] = remote(column_block, column_block, send2.at[1, d], recv2.at[1, d], at_x(d))
        second[0, d].start()
        second[1, d].start()
    shared = []
    for part, block in ((0, row_block), (1, column_block)):
        copy = remote(block, block, core_send.at[part, 0], core_recv.at[part, 0], other)
        copy.start()
        shared.append(copy)
    for d in (1, 3, 2):
        second[0, d].wait_recv()
        block = kv_ref.at[0, :, lax.rem(y + 4 - d, 4), k]
        copy = remote(block, block, core_send.at[0, d], core_recv.at[0, d], other)
        copy.start()
        shared.append(copy)
        second[1, d].wait_recv()
        block = kv_ref.at[1, lax.rem(x + 4 - d, 4), :, k]
        copy = remote(block, block, core_send.at[1, d], core_recv.at[1, d], other)
        copy.start()
        shared.append(copy)
    for copy in shared:
        copy.wait()
    for copy in list(first.values()) + list(second.values()):
        copy.wait_send()


def gather_pages(page_cache):
    rows = page_cache.shape[1]
    return pl.pallas_call(
        gather_kernel,
        out_shape=jax.ShapeDtypeStruct((2, 4, 4, 2, rows, HD), jnp.bfloat16),
        in_specs=[pl.BlockSpec(memory_space=pl.ANY)],
        out_specs=pl.BlockSpec(memory_space=pl.ANY),
        scratch_shapes=[pltpu.SemaphoreType.DMA(())]
        + [pltpu.SemaphoreType.DMA((2, 4))] * 6,
        compiler_params=pltpu.CompilerParams(collective_id=0, has_side_effects=True),
        name="gather_pages",
    )(page_cache)


def attention_kernel(
    slot_ref, parent_ref, count_ref, lost_ref, q_ref, new_ref, kv_ref, out_ref, keys, values, query, top, total
):
    pages_here = q_ref.shape[0] // PAGE
    scale = math.log2(math.e) / math.sqrt(HD)
    base = lax.axis_index("ctx") * pages_here
    token = lax.broadcasted_iota(jnp.int32, (PAGE, HD), 0)
    nt = (((1,), (1,)), ((), ()))

    def one_lost(j, unused):
        rows = pl.ds(pl.multiple_of(j * PAGE, PAGE), PAGE)

        def append(state):
            page, filled = state
            count = count_ref[page]
            at = pl.ds(pl.multiple_of(slot_ref[page] * PAGE, PAGE), PAGE)
            to = pl.ds(pl.multiple_of(filled, 16), PAGE)
            kept = token < count
            key = kv_ref[0, at, :].astype(jnp.float32)
            keys[to, :] = jnp.where(kept, key, key[:1, :]).astype(jnp.bfloat16)
            value = kv_ref[1, at, :].astype(jnp.float32)
            values[to, :HD] = jnp.where(kept, value, 0.0).astype(jnp.bfloat16)
            values[to, HD:] = kept.astype(jnp.float32).astype(jnp.bfloat16)
            return parent_ref[page], filled + ((count + 15) // 16) * 16

        unused_page, filled = lax.while_loop(
            lambda state: state[0] >= 0, append, (lost_ref[base + j], jnp.int32(0))
        )
        tail = pl.ds(pl.multiple_of(filled, 16), CHUNK)
        keys[tail, :] = jnp.broadcast_to(keys[:1, :].astype(jnp.float32), (CHUNK, HD)).astype(jnp.bfloat16)
        values[tail, :] = jnp.zeros((CHUNK, 2 * HD), jnp.bfloat16)
        for h in range(GROUP):
            query[h * PAGE : (h + 1) * PAGE, :] = q_ref[rows, h * HD : (h + 1) * HD]

        fresh = lax.dot_general(query[...], new_ref[0, rows, :], nt, preferred_element_type=jnp.float32) * scale
        q_at = lax.rem(lax.broadcasted_iota(jnp.int32, (GROUP * PAGE, PAGE), 0), PAGE)
        k_at = lax.broadcasted_iota(jnp.int32, (GROUP * PAGE, PAGE), 1)
        seen = k_at <= q_at
        fresh = jnp.where(seen, fresh, -1e30)
        highest = jnp.max(fresh, axis=1, keepdims=True)
        weight = jnp.where(seen, jnp.exp2(fresh - highest), 0.0).astype(jnp.bfloat16)
        with_ones = jnp.concatenate([new_ref[1, rows, :], jnp.ones((PAGE, HD), jnp.bfloat16)], axis=1)
        top[...] = jnp.broadcast_to(highest, top.shape)
        total[...] = jnp.dot(weight, with_ones, preferred_element_type=jnp.float32)

        def one_chunk(n, unused):
            at = pl.ds(pl.multiple_of(n * CHUNK, CHUNK), CHUNK)
            score = lax.dot_general(query[...], keys[at, :], nt, preferred_element_type=jnp.float32) * scale
            before = top[:, :1]
            highest = jnp.maximum(before, jnp.max(score, axis=1, keepdims=True))
            weight = jnp.exp2(score - highest).astype(jnp.bfloat16)
            factor = jnp.exp2(before - highest)
            top[...] = jnp.broadcast_to(highest, top.shape)
            total[...] = total[...] * factor + jnp.dot(weight, values[at, :], preferred_element_type=jnp.float32)
            return unused

        lax.fori_loop(0, (filled + CHUNK - 1) // CHUNK, one_chunk, 0)
        for h in range(GROUP):
            block = total[h * PAGE : (h + 1) * PAGE, :]
            out_ref[rows, h * HD : (h + 1) * HD] = (block[:, :HD] / block[:, HD:]).astype(jnp.bfloat16)
        return unused

    lax.fori_loop(0, pages_here, one_lost, 0)


def attend(queries, new_kv, kv, page_slot, parent, valid_count, lost_parent):
    rows = kv.shape[1]
    smem = pl.BlockSpec(memory_space=pltpu.SMEM)
    vmem = pl.BlockSpec(memory_space=pltpu.VMEM)
    return pl.pallas_call(
        attention_kernel,
        out_shape=jax.ShapeDtypeStruct(queries.shape, jnp.bfloat16),
        in_specs=[smem] * 4 + [vmem] * 3,
        out_specs=vmem,
        scratch_shapes=[
            pltpu.VMEM((rows + CHUNK, HD), jnp.bfloat16),
            pltpu.VMEM((rows + CHUNK, 2 * HD), jnp.bfloat16),
            pltpu.VMEM((GROUP * PAGE, HD), jnp.bfloat16),
            pltpu.VMEM((GROUP * PAGE, HD), jnp.float32),
            pltpu.VMEM((GROUP * PAGE, 2 * HD), jnp.float32),
        ],
        compiler_params=pltpu.CompilerParams(vmem_limit_bytes=VMEM_LIMIT),
        name="attend",
    )(page_slot, parent, valid_count, lost_parent, queries, new_kv, kv)


ORDER = [(0, 0), (1, 0), (0, 1), (1, 1), (0, 2), (1, 2)]
for _s in range(8):
    ORDER += [(2, _s), (3, _s)]
    if _s + 3 < 8:
        ORDER += [(0, _s + 3), (1, _s + 3)]


def project_kernel(
    att_ref, w_ref, out_ref, peers, outgoing, incoming, final, a_send, a_recv, z_send, z_recv, f_send, f_recv
):
    x, y, k, t = place()
    y_other = y + 1 - 2 * lax.rem(y, 2)
    mine = lax.rem(y, 2) * 2 + k
    holder = {
        1: (ctx_of(x, y, 1 - k), t),
        2: (ctx_of(x, y_other, k), t),
        3: (ctx_of(x, y_other, 1 - k), t),
    }
    here = ctx_of(x, y, k)
    barrier = pltpu.get_barrier_semaphore()
    for device in list(holder.values()) + [(here, lax.rem(t + 1, 8)), (here, lax.rem(t + 7, 8))]:
        pl.semaphore_signal(barrier, inc=1, device_id=device, device_id_type=MESH)
    pl.semaphore_wait(barrier, 5)

    def remote(src, dst, send, recv, device):
        copy = pltpu.make_async_remote_copy(src, dst, send, recv, device_id=device, device_id_type=MESH)
        copy.start()
        return copy

    shares = {
        1: remote(att_ref, peers.at[0], a_send.at[0], a_recv.at[0], holder[1]),
        2: remote(att_ref, peers.at[1], a_send.at[1], a_recv.at[1], holder[2]),
    }
    step_of = {0: 1 - 2 * k, 1: 2 * k - 1, 2: 1 - 2 * k, 3: 2 * k - 1}
    columns = w_ref.shape[1]
    nt = (((1,), (1,)), ((), ()))
    hops = {}
    finals = []
    for block, s in ORDER:
        if s == 0 and block > 0:
            shares[block].wait_recv()
            if block == 2:
                shares[3] = remote(peers.at[1], peers.at[2], a_send.at[2], a_recv.at[2], holder[1])
        step = step_of[block]
        target = lax.rem(t - step * (1 + s) + 16, 8)
        rows = att_ref[...] if block == 0 else peers[block - 1]
        term = lax.dot_general(w_ref[target], rows, nt, preferred_element_type=jnp.float32)
        if s > 0:
            hops[block, s - 1].wait_recv()
            term = term + incoming[block, s - 1].astype(jnp.float32)
        term = term.astype(jnp.bfloat16)
        if s < 7:
            outgoing[block, s] = term
            hops[block, s] = remote(
                outgoing.at[block, s],
                incoming.at[block, s],
                z_send.at[block, s],
                z_recv.at[block, s],
                (here, lax.rem(t + step + 8, 8)),
            )
        else:
            spot = pl.ds(pl.multiple_of(mine * columns, 16), columns)
            if block == 0:
                out_ref[spot, :] = term
            else:
                final[block - 1] = term
                finals.append(
                    remote(
                        final.at[block - 1],
                        out_ref.at[spot, :],
                        f_send.at[block - 1],
                        f_recv.at[block - 1],
                        holder[block],
                    )
                )
    for copy in finals:
        copy.wait()
    for copy in list(shares.values()) + list(hops.values()):
        copy.wait_send()


def project(attended, weights):
    rows, depth = attended.shape
    parts, columns, _ = weights.shape
    vmem = pl.BlockSpec(memory_space=pltpu.VMEM)
    return pl.pallas_call(
        project_kernel,
        out_shape=jax.ShapeDtypeStruct((4 * columns, rows), jnp.bfloat16),
        in_specs=[vmem, vmem],
        out_specs=vmem,
        scratch_shapes=[
            pltpu.VMEM((3, rows, depth), jnp.bfloat16),
            pltpu.VMEM((4, 7, columns, rows), jnp.bfloat16),
            pltpu.VMEM((4, 7, columns, rows), jnp.bfloat16),
            pltpu.VMEM((3, columns, rows), jnp.bfloat16),
            pltpu.SemaphoreType.DMA((3,)),
            pltpu.SemaphoreType.DMA((3,)),
            pltpu.SemaphoreType.DMA((4, 7)),
            pltpu.SemaphoreType.DMA((4, 7)),
            pltpu.SemaphoreType.DMA((3,)),
            pltpu.SemaphoreType.DMA((3,)),
        ],
        compiler_params=pltpu.CompilerParams(
            collective_id=1, has_side_effects=True, vmem_limit_bytes=VMEM_LIMIT
        ),
        name="project",
    )(attended, weights)


def weight_groups():
    return [
        [(x * 4 + high * 2 + low) * 2 + k for x in range(4) for high in range(2)]
        for low in range(2)
        for k in range(2)
    ]


def per_device(
    queries, new_kv, page_cache, out_weight, page_slot, parent, valid_count, lost_parent
):
    weights = lax.all_gather(out_weight.T, "ctx", axis_index_groups=weight_groups())
    kv = gather_pages(page_cache).reshape(2, -1, HD)
    attended = attend(queries, new_kv, kv, page_slot, parent, valid_count, lost_parent)
    return project(attended, weights).T


def solution(mesh):
    return jax.shard_map(
        per_device,
        mesh=mesh,
        in_specs=(
            P("ctx", "tp"),
            P(None, "ctx", "tp"),
            P(None, "ctx", "tp"),
            P("tp", "ctx"),
            P(),
            P(),
            P(),
            P(),
        ),
        out_specs=P("ctx", "tp"),
        check_vma=False,
    )
```

```python
import math

import jax
import jax.numpy as jnp
from jax import lax
from jax.experimental import pallas as pl
from jax.experimental.pallas import tpu as pltpu
from jax.sharding import PartitionSpec as P

HEADS = 56
KV_HEADS = 8
HD = 128
PAGE = 128
GROUP = HEADS // KV_HEADS
CHUNK = 512
MESH = pl.DeviceIdType.MESH
VMEM_LIMIT = 28 * 2**20


def place():
    c = lax.axis_index("ctx")
    return lax.div(c, 8), lax.rem(lax.div(c, 2), 4), lax.rem(c, 2), lax.axis_index("tp")


def ctx_of(x, y, k):
    return (x * 4 + y) * 2 + k


def gather_kernel(page_ref, w_ref, kv_ref, wall_ref, own_sem, send_sem, recv_sem):
    x, y, k, t = place()

    def at_x(d):
        return (ctx_of(lax.rem(x + d, 4), y, k), t)

    def at_y(d):
        return (ctx_of(x, lax.rem(y + d, 4), k), t)

    other = (ctx_of(x, y, 1 - k), t)
    barrier = pltpu.get_barrier_semaphore()
    for device in (at_x(1), at_x(2), at_x(3), at_y(1), at_y(3), other):
        pl.semaphore_signal(barrier, inc=1, device_id=device, device_id_type=MESH)
    own = [
        pltpu.make_async_copy(page_ref, kv_ref.at[:, x, y, k], own_sem.at[0]),
        pltpu.make_async_copy(w_ref, wall_ref.at[x], own_sem.at[1]),
    ]
    for copy in own:
        copy.start()
    pl.semaphore_wait(barrier, 6)

    copies = []

    def remote(src, dst, device):
        n = len(copies)
        copy = pltpu.make_async_remote_copy(
            src, dst, send_sem.at[n], recv_sem.at[n], device_id=device, device_id_type=MESH
        )
        copy.start()
        copies.append(copy)
        return copy

    def piece(dx, dy):
        return kv_ref.at[:, lax.rem(x + dx, 4), lax.rem(y + dy, 4), k]

    def half(part, dx, dy):
        return kv_ref.at[part, lax.rem(x + dx, 4), lax.rem(y + dy, 4), k]

    home = piece(0, 0)
    along = {d: remote(page_ref, home, at_x(d)) for d in (1, 3, 2)}
    up = {0: remote(page_ref, home, at_y(1))}
    down = {0: remote(page_ref, home, at_y(3))}
    shared = [remote(page_ref, home, other)]
    for d in (1, 3, 2):
        along[d].wait_recv()
        here = piece(4 - d, 0)
        up[d] = remote(here, here, at_y(1))
        down[d] = remote(here, here, at_y(3))
        shared.append(remote(here, here, other))
    right = remote(w_ref, wall_ref.at[x], at_x(1))
    left = remote(w_ref, wall_ref.at[x], at_x(3))
    far = {}
    far_w = []
    middle = w_ref.shape[0] // 2
    for d in (0, 1, 3, 2):
        dx = (4 - d) % 4
        up[d].wait_recv()
        here = half(0, dx, 3)
        far[0, d] = remote(here, here, at_y(1))
        shared.append(remote(piece(dx, 3), piece(dx, 3), other))
        down[d].wait_recv()
        here = half(1, dx, 1)
        far[1, d] = remote(here, here, at_y(3))
        shared.append(remote(piece(dx, 1), piece(dx, 1), other))
        if d == 3:
            right.wait_recv()
            here = wall_ref.at[lax.rem(x + 3, 4), pl.ds(0, middle)]
            far_w.append(remote(here, here, at_x(1)))
            left.wait_recv()
            here = wall_ref.at[lax.rem(x + 1, 4), pl.ds(middle, middle)]
            far_w.append(remote(here, here, at_x(3)))
    for d in (0, 1, 3, 2):
        far[0, d].wait_recv()
        far[1, d].wait_recv()
        here = piece((4 - d) % 4, 2)
        shared.append(remote(here, here, other))
    for copy in far_w:
        copy.wait_recv()
    for copy in shared:
        copy.wait_recv()
    for copy in copies:
        copy.wait_send()
    for copy in own:
        copy.wait()


GATHER_COPIES = 6 + 9 + 2 + 16 + 2 + 4


def gather_pages(page_cache, weights):
    rows = page_cache.shape[1]
    anywhere = pl.BlockSpec(memory_space=pl.ANY)
    return pl.pallas_call(
        gather_kernel,
        out_shape=(
            jax.ShapeDtypeStruct((2, 4, 4, 2, rows, HD), jnp.bfloat16),
            jax.ShapeDtypeStruct((4,) + weights.shape, jnp.bfloat16),
        ),
        in_specs=[anywhere, anywhere],
        out_specs=(anywhere, anywhere),
        scratch_shapes=[
            pltpu.SemaphoreType.DMA((2,)),
            pltpu.SemaphoreType.DMA((GATHER_COPIES,)),
            pltpu.SemaphoreType.DMA((GATHER_COPIES,)),
        ],
        compiler_params=pltpu.CompilerParams(collective_id=0, has_side_effects=True),
        name="gather_pages",
    )(page_cache, weights)


LANES = ((0, 256), (256, 256), (512, 256), (768, 128))
EXTRA = 16


def attention_kernel(
    slot_ref, parent_ref, count_ref, lost_ref, q_ref, new_ref, kv_ref, out_ref, keys, values, query, top, total
):
    pages_here = q_ref.shape[0] // PAGE
    scale = math.log2(math.e) / math.sqrt(HD)
    base = lax.axis_index("ctx") * pages_here
    token = lax.broadcasted_iota(jnp.int32, (16, HD), 0)
    nt = (((1,), (1,)), ((), ()))

    def transposed(block):
        return block.T[: HD + EXTRA]

    def one_lost(j, unused):
        rows = pl.ds(pl.multiple_of(j * PAGE, PAGE), PAGE)

        def append(state):
            page, filled = state
            count = count_ref[page]
            first = slot_ref[page] * PAGE
            at = pl.ds(pl.multiple_of(first, PAGE), PAGE)
            to = pl.ds(pl.multiple_of(filled, 16), PAGE)
            keys[to, :] = kv_ref[0, at, :]
            values[to, :HD] = kv_ref[1, at, :]
            values[to, HD:] = jnp.ones((PAGE, HD), jnp.bfloat16)
            last = ((count - 1) // 16) * 16
            kept = token + last < count
            at = pl.ds(pl.multiple_of(first + last, 16), 16)
            to = pl.ds(pl.multiple_of(filled + last, 16), 16)
            lead = kv_ref[0, pl.ds(pl.multiple_of(first, PAGE), 16), :].astype(jnp.float32)[:1, :]
            keys[to, :] = jnp.where(kept, kv_ref[0, at, :].astype(jnp.float32), lead).astype(jnp.bfloat16)
            values[to, :HD] = jnp.where(kept, kv_ref[1, at, :].astype(jnp.float32), 0.0).astype(jnp.bfloat16)
            values[to, HD:] = kept.astype(jnp.float32).astype(jnp.bfloat16)
            return parent_ref[page], filled + last + 16

        unused_page, filled = lax.while_loop(
            lambda state: state[0] >= 0, append, (lost_ref[base + j], jnp.int32(0))
        )
        tail = pl.ds(pl.multiple_of(filled, 16), CHUNK)
        lead = keys[:16, :].astype(jnp.float32)[:1, :]
        keys[tail, :] = jnp.broadcast_to(lead, (CHUNK, HD)).astype(jnp.bfloat16)
        values[tail, :] = jnp.zeros((CHUNK, 2 * HD), jnp.bfloat16)
        for h in range(GROUP):
            query[h * PAGE : (h + 1) * PAGE, :] = q_ref[rows, h * HD : (h + 1) * HD]

        with_ones = transposed(
            jnp.concatenate([new_ref[1, rows, :], jnp.ones((PAGE, HD), jnp.bfloat16)], axis=1)
        )
        for start, width in LANES:
            lanes = pl.ds(start, width)
            score = lax.dot_general(
                new_ref[0, rows, :], query[lanes, :], nt, preferred_element_type=jnp.float32
            )
            k_at = lax.broadcasted_iota(jnp.int32, (PAGE, width), 0)
            q_at = lax.broadcasted_iota(jnp.int32, (PAGE, width), 1) % PAGE
            seen = k_at <= q_at
            score = jnp.where(seen, score, -1e30)
            highest = jnp.max(score, axis=0, keepdims=True)
            weight = jnp.where(seen, jnp.exp2(score * scale - highest * scale), 0.0).astype(jnp.bfloat16)
            top[:, lanes] = jnp.broadcast_to(highest, (8, width))
            total[:, lanes] = jnp.dot(with_ones, weight, preferred_element_type=jnp.float32)

        def one_chunk(n, unused):
            at = pl.ds(pl.multiple_of(n * CHUNK, CHUNK), CHUNK)
            key = keys[at, :]
            value = transposed(values[at, :])
            for start, width in LANES:
                lanes = pl.ds(start, width)
                score = lax.dot_general(key, query[lanes, :], nt, preferred_element_type=jnp.float32)
                before = top[:1, lanes]
                highest = jnp.maximum(before, jnp.max(score, axis=0, keepdims=True))
                weight = jnp.exp2(score * scale - highest * scale).astype(jnp.bfloat16)
                factor = jnp.exp2((before - highest) * scale)
                top[:, lanes] = jnp.broadcast_to(highest, (8, width))
                total[:, lanes] = total[:, lanes] * factor + jnp.dot(
                    value, weight, preferred_element_type=jnp.float32
                )
            return unused

        lax.fori_loop(0, (filled + CHUNK - 1) // CHUNK, one_chunk, 0)
        for h in range(GROUP):
            lanes = pl.ds(h * PAGE, PAGE)
            out_ref[h * HD : (h + 1) * HD, rows] = (total[:HD, lanes] / total[HD : HD + 1, lanes]).astype(
                jnp.bfloat16
            )
        return unused

    lax.fori_loop(0, pages_here, one_lost, 0)


def attend(queries, new_kv, kv, page_slot, parent, valid_count, lost_parent):
    rows = kv.shape[1]
    smem = pl.BlockSpec(memory_space=pltpu.SMEM)
    vmem = pl.BlockSpec(memory_space=pltpu.VMEM)
    return pl.pallas_call(
        attention_kernel,
        out_shape=jax.ShapeDtypeStruct(queries.shape[::-1], jnp.bfloat16),
        in_specs=[smem] * 4 + [vmem] * 3,
        out_specs=vmem,
        scratch_shapes=[
            pltpu.VMEM((rows + CHUNK, HD), jnp.bfloat16),
            pltpu.VMEM((rows + CHUNK, 2 * HD), jnp.bfloat16),
            pltpu.VMEM((GROUP * PAGE, HD), jnp.bfloat16),
            pltpu.VMEM((8, GROUP * PAGE), jnp.float32),
            pltpu.VMEM((HD + EXTRA, GROUP * PAGE), jnp.float32),
        ],
        compiler_params=pltpu.CompilerParams(vmem_limit_bytes=VMEM_LIMIT),
        name="attend",
    )(page_slot, parent, valid_count, lost_parent, queries, new_kv, kv)


OWN = [(0, 0), (0, 1)]
NEAR = [(1, 0), (3, 0), (1, 1), (3, 1)]
FAR = [(2, 0), (2, 1)]
WAVES = []
for _w in range(6):
    for _delay, _blocks in ((0, OWN), (1, NEAR), (2, FAR)):
        if 0 <= _w - _delay < 4:
            WAVES += [(_block, _w - _delay) for _block in _blocks]


def project_kernel(
    att_ref, w_ref, out_ref, peers, outgoing, incoming, a_send, a_recv, z_send, z_recv, f_send, f_recv
):
    x, y, k, t = place()
    here = ctx_of(x, y, k)

    def holder(dy, dk):
        return (ctx_of(x, lax.rem(y + dy, 4), k if dk == 0 else 1 - k), t)

    columns = w_ref.shape[1]
    width = att_ref.shape[1] // 2
    sides = (pl.ds(0, width), pl.ds(width, width))
    mine = lax.rem(y, 2) * 2 + k
    late = lax.rem(t + lax.div(y, 2), 2)
    barrier = pltpu.get_barrier_semaphore()
    others = [(dy, dk) for dy in range(4) for dk in range(2) if (dy, dk) != (0, 0)]
    for device in [holder(dy, dk) for dy, dk in others] + [(here, lax.rem(t + 1, 8)), (here, lax.rem(t + 7, 8))]:
        pl.semaphore_signal(barrier, inc=1, device_id=device, device_id_type=MESH)
    pl.semaphore_wait(barrier, 9)

    a_copies = []

    def share(src, dst, device):
        n = len(a_copies)
        copy = pltpu.make_async_remote_copy(
            src, dst, a_send.at[n], a_recv.at[n], device_id=device, device_id_type=MESH
        )
        copy.start()
        a_copies.append(copy)
        return copy

    core = {0: share(att_ref, peers.at[0, 1], holder(0, 1))}
    near = {3: share(att_ref, peers.at[3, 0], holder(1, 0)), 1: share(att_ref, peers.at[1, 0], holder(3, 0))}
    far = {}

    def need(dy, dk):
        if (dy, dk) == (0, 0):
            return
        if dk == 1:
            core[dy].wait_recv()
        elif dy in near:
            near[dy].wait_recv()
            side = 0 if dy == 3 else 1
            far[side] = share(
                peers.at[dy, 0, :, sides[side]],
                peers.at[2, 0, :, sides[side]],
                holder(1 if dy == 3 else 3, 0),
            )
            core[dy] = share(peers.at[dy, 0], peers.at[dy, 1], holder(0, 1))
        else:
            far[0].wait_recv()
            far[1].wait_recv()
            core[2] = share(peers.at[2, 0], peers.at[2, 1], holder(0, 1))

    def hop(block, i, side):
        dy, dk = block
        step = (1 - 2 * k) * (1 - 2 * dk)
        slot = i + 1 - late
        return pltpu.make_async_remote_copy(
            outgoing.at[dy, dk, i, :, sides[side]],
            incoming.at[dy, dk, slot, :, sides[side]],
            z_send.at[dy, dk, i, side],
            z_recv.at[dy, dk, slot, side],
            device_id=(here, lax.rem(t + step + 8, 8)),
            device_id_type=MESH,
        )

    def arrived(block, i, side):
        dy, dk = block
        spot = incoming.at[dy, dk, i, :, sides[side]]
        pltpu.make_async_copy(spot, spot, z_recv.at[dy, dk, i, side]).wait()

    spot = pl.ds(pl.multiple_of(mine * columns, 16), columns)

    def result(block):
        dy, dk = block
        return pltpu.make_async_remote_copy(
            outgoing.at[dy, dk, 3],
            out_ref.at[spot, :],
            f_send.at[dy, dk],
            f_recv.at[mine],
            device_id=holder(dy, dk),
            device_id_type=MESH,
        )

    for block, i in WAVES:
        dy, dk = block
        if i == 0:
            need(dy, dk)
        step = (1 - 2 * k) * (1 - 2 * dk)
        target = lax.rem(t - step * (2 * i + 2 - late) + 16, 8)
        rows = att_ref[...] if block == (0, 0) else peers[dy, dk]
        term = jnp.dot(w_ref[lax.div(target, 2)], rows, preferred_element_type=jnp.float32)

        def add_and_send(block=block, i=i, term=term, send=True):
            dy, dk = block
            for side in (0, 1):
                arrived(block, i, side)
                cut = slice(side * width, (side + 1) * width)
                total = term[:, cut] + incoming[dy, dk, i, :, sides[side]].astype(jnp.float32)
                outgoing[dy, dk, i, :, sides[side]] = total.astype(jnp.bfloat16)
                if send:
                    hop(block, i, side).start()

        if i == 0:

            @pl.when(late == 1)
            def _(block=block, i=i, term=term):
                dy, dk = block
                outgoing[dy, dk, i] = term.astype(jnp.bfloat16)
                hop(block, i, 0).start()
                hop(block, i, 1).start()

            pl.when(late == 0)(add_and_send)
        elif i < 3:
            add_and_send()
        else:
            pl.when(late == 1)(add_and_send)

            @pl.when(late == 0)
            def _(block=block, i=i, term=term, add=add_and_send):
                dy, dk = block
                add(block, i, term, False)
                if block == (0, 0):
                    out_ref[spot, :] = outgoing[0, 0, 3]
                else:
                    result(block).start()

    for n in range(4):

        @pl.when((late == 1) | (mine != n))
        def _(n=n):
            landed = out_ref.at[pl.ds(n * columns, columns), :]
            pltpu.make_async_copy(landed, landed, f_recv.at[n]).wait()

    for copy in a_copies:
        copy.wait_send()
    for block in OWN + NEAR + FAR:
        for i in range(3):
            hop(block, i, 0).wait_send()
            hop(block, i, 1).wait_send()

        @pl.when(late == 1)
        def _(block=block):
            hop(block, 3, 0).wait_send()
            hop(block, 3, 1).wait_send()

        if block != (0, 0):

            @pl.when(late == 0)
            def _(block=block):
                result(block).wait_send()


def project(attended, weights):
    depth, rows = attended.shape
    columns = weights.shape[1]
    vmem = pl.BlockSpec(memory_space=pltpu.VMEM)
    return pl.pallas_call(
        project_kernel,
        out_shape=jax.ShapeDtypeStruct((4 * columns, rows), jnp.bfloat16),
        in_specs=[vmem, vmem],
        out_specs=vmem,
        scratch_shapes=[
            pltpu.VMEM((4, 2, depth, rows), jnp.bfloat16),
            pltpu.VMEM((4, 2, 4, columns, rows), jnp.bfloat16),
            pltpu.VMEM((4, 2, 4, columns, rows), jnp.bfloat16),
            pltpu.SemaphoreType.DMA((8,)),
            pltpu.SemaphoreType.DMA((8,)),
            pltpu.SemaphoreType.DMA((4, 2, 4, 2)),
            pltpu.SemaphoreType.DMA((4, 2, 4, 2)),
            pltpu.SemaphoreType.DMA((4, 2)),
            pltpu.SemaphoreType.DMA((4,)),
        ],
        compiler_params=pltpu.CompilerParams(
            collective_id=1, has_side_effects=True, vmem_limit_bytes=VMEM_LIMIT
        ),
        name="project",
    )(attended, weights)


def per_device(
    queries, new_kv, page_cache, out_weight, page_slot, parent, valid_count, lost_parent
):
    kv, weights = gather_pages(page_cache, out_weight.T)
    kv = kv.reshape(2, -1, HD)
    attended = attend(queries, new_kv, kv, page_slot, parent, valid_count, lost_parent)
    return project(attended, weights).T


def solution(mesh):
    return jax.shard_map(
        per_device,
        mesh=mesh,
        in_specs=(
            P("ctx", "tp"),
            P(None, "ctx", "tp"),
            P(None, "ctx", "tp"),
            P("tp", "ctx"),
            P(),
            P(),
            P(),
            P(),
        ),
        out_specs=P("ctx", "tp"),
        check_vma=False,
    )
```

```python
import math

import jax
import jax.numpy as jnp
from jax import lax
from jax.experimental import pallas as pl
from jax.experimental.pallas import tpu as pltpu
from jax.sharding import PartitionSpec as P

HEADS = 56
KV_HEADS = 8
HD = 128
PAGE = 128
GROUP = HEADS // KV_HEADS
CHUNK = 768
MESH = pl.DeviceIdType.MESH
VMEM_LIMIT = 56 * 2**20


def place():
    c = lax.axis_index("ctx")
    return lax.div(c, 8), lax.rem(lax.div(c, 2), 4), lax.rem(c, 2), lax.axis_index("tp")


def ctx_of(x, y, k):
    return (x * 4 + y) * 2 + k


def gather_kernel(page_ref, w_ref, kv_ref, wall_ref, own_sem, send_sem, recv_sem):
    x, y, k, t = place()

    def at_x(d):
        return (ctx_of(lax.rem(x + d, 4), y, k), t)

    def at_y(d):
        return (ctx_of(x, lax.rem(y + d, 4), k), t)

    other = (ctx_of(x, y, 1 - k), t)
    barrier = pltpu.get_barrier_semaphore()
    for device in (at_x(1), at_x(2), at_x(3), at_y(1), at_y(3), other):
        pl.semaphore_signal(barrier, inc=1, device_id=device, device_id_type=MESH)
    own = [
        pltpu.make_async_copy(page_ref, kv_ref.at[:, x, y, k], own_sem.at[0]),
        pltpu.make_async_copy(w_ref, wall_ref.at[x], own_sem.at[1]),
    ]
    for copy in own:
        copy.start()
    pl.semaphore_wait(barrier, 6)

    copies = []

    def remote(src, dst, device):
        n = len(copies)
        copy = pltpu.make_async_remote_copy(
            src, dst, send_sem.at[n], recv_sem.at[n], device_id=device, device_id_type=MESH
        )
        copy.start()
        copies.append(copy)
        return copy

    def piece(dx, dy):
        return kv_ref.at[:, lax.rem(x + dx, 4), lax.rem(y + dy, 4), k]

    def half(part, dx, dy):
        return kv_ref.at[part, lax.rem(x + dx, 4), lax.rem(y + dy, 4), k]

    home = piece(0, 0)
    along = {d: remote(page_ref, home, at_x(d)) for d in (1, 3, 2)}
    up = {0: remote(page_ref, home, at_y(1))}
    down = {0: remote(page_ref, home, at_y(3))}
    shared = [remote(page_ref, home, other)]
    for d in (1, 3, 2):
        along[d].wait_recv()
        here = piece(4 - d, 0)
        up[d] = remote(here, here, at_y(1))
        down[d] = remote(here, here, at_y(3))
        shared.append(remote(here, here, other))
    right = remote(w_ref, wall_ref.at[x], at_x(1))
    left = remote(w_ref, wall_ref.at[x], at_x(3))
    far = {}
    far_w = []
    middle = w_ref.shape[0] // 2
    for d in (0, 1, 3, 2):
        dx = (4 - d) % 4
        up[d].wait_recv()
        here = half(0, dx, 3)
        far[0, d] = remote(here, here, at_y(1))
        shared.append(remote(piece(dx, 3), piece(dx, 3), other))
        down[d].wait_recv()
        here = half(1, dx, 1)
        far[1, d] = remote(here, here, at_y(3))
        shared.append(remote(piece(dx, 1), piece(dx, 1), other))
        if d == 3:
            right.wait_recv()
            here = wall_ref.at[lax.rem(x + 3, 4), pl.ds(0, middle)]
            far_w.append(remote(here, here, at_x(1)))
            left.wait_recv()
            here = wall_ref.at[lax.rem(x + 1, 4), pl.ds(middle, middle)]
            far_w.append(remote(here, here, at_x(3)))
    for d in (0, 1, 3, 2):
        far[0, d].wait_recv()
        far[1, d].wait_recv()
        here = piece((4 - d) % 4, 2)
        shared.append(remote(here, here, other))
    for copy in far_w:
        copy.wait_recv()
    for copy in shared:
        copy.wait_recv()
    for copy in copies:
        copy.wait_send()
    for copy in own:
        copy.wait()


GATHER_COPIES = 6 + 9 + 2 + 16 + 2 + 4


def gather_pages(page_cache, weights):
    rows = page_cache.shape[1]
    anywhere = pl.BlockSpec(memory_space=pl.ANY)
    return pl.pallas_call(
        gather_kernel,
        out_shape=(
            jax.ShapeDtypeStruct((2, 4, 4, 2, rows, HD), jnp.bfloat16),
            jax.ShapeDtypeStruct((4,) + weights.shape, jnp.bfloat16),
        ),
        in_specs=[anywhere, anywhere],
        out_specs=(anywhere, anywhere),
        scratch_shapes=[
            pltpu.SemaphoreType.DMA((2,)),
            pltpu.SemaphoreType.DMA((GATHER_COPIES,)),
            pltpu.SemaphoreType.DMA((GATHER_COPIES,)),
        ],
        compiler_params=pltpu.CompilerParams(collective_id=0, has_side_effects=True),
        name="gather_pages",
    )(page_cache, weights)


LANES = ((0, GROUP * PAGE),)
EXTRA = 16


def attention_kernel(
    slot_ref, parent_ref, count_ref, lost_ref, q_ref, new_ref, kv_ref, out_ref, keys, values, query, top, total
):
    pages_here = q_ref.shape[0] // PAGE
    scale = math.log2(math.e) / math.sqrt(HD)
    base = lax.axis_index("ctx") * pages_here
    token = lax.broadcasted_iota(jnp.int32, (16, HD), 0)
    nt = (((1,), (1,)), ((), ()))

    def transposed(block):
        return block.T[: HD + EXTRA]

    def one_lost(j, unused):
        rows = pl.ds(pl.multiple_of(j * PAGE, PAGE), PAGE)

        def append(state):
            page, filled = state
            count = count_ref[page]
            first = slot_ref[page] * PAGE
            at = pl.ds(pl.multiple_of(first, PAGE), PAGE)
            to = pl.ds(pl.multiple_of(filled, 16), PAGE)
            keys[to, :] = kv_ref[0, at, :]
            values[to, :HD] = kv_ref[1, at, :]
            values[to, HD:] = jnp.ones((PAGE, HD), jnp.bfloat16)
            last = ((count - 1) // 16) * 16
            kept = token + last < count
            at = pl.ds(pl.multiple_of(first + last, 16), 16)
            to = pl.ds(pl.multiple_of(filled + last, 16), 16)
            lead = kv_ref[0, pl.ds(pl.multiple_of(first, PAGE), 16), :].astype(jnp.float32)[:1, :]
            keys[to, :] = jnp.where(kept, kv_ref[0, at, :].astype(jnp.float32), lead).astype(jnp.bfloat16)
            values[to, :HD] = jnp.where(kept, kv_ref[1, at, :].astype(jnp.float32), 0.0).astype(jnp.bfloat16)
            values[to, HD:] = kept.astype(jnp.float32).astype(jnp.bfloat16)
            return parent_ref[page], filled + last + 16

        unused_page, filled = lax.while_loop(
            lambda state: state[0] >= 0, append, (lost_ref[base + j], jnp.int32(0))
        )
        tail = pl.ds(pl.multiple_of(filled, 16), CHUNK)
        lead = keys[:16, :].astype(jnp.float32)[:1, :]
        keys[tail, :] = jnp.broadcast_to(lead, (CHUNK, HD)).astype(jnp.bfloat16)
        values[tail, :] = jnp.zeros((CHUNK, 2 * HD), jnp.bfloat16)
        for h in range(GROUP):
            query[h * PAGE : (h + 1) * PAGE, :] = q_ref[rows, h * HD : (h + 1) * HD]

        with_ones = transposed(
            jnp.concatenate([new_ref[1, rows, :], jnp.ones((PAGE, HD), jnp.bfloat16)], axis=1)
        )
        for start, width in LANES:
            lanes = pl.ds(start, width)
            score = lax.dot_general(
                new_ref[0, rows, :], query[lanes, :], nt, preferred_element_type=jnp.float32
            )
            k_at = lax.broadcasted_iota(jnp.int32, (PAGE, width), 0)
            q_at = lax.broadcasted_iota(jnp.int32, (PAGE, width), 1) % PAGE
            seen = k_at <= q_at
            score = jnp.where(seen, score, -1e30)
            highest = jnp.max(score, axis=0, keepdims=True)
            weight = jnp.where(seen, jnp.exp2(score * scale - highest * scale), 0.0).astype(jnp.bfloat16)
            top[:, lanes] = jnp.broadcast_to(highest, (8, width))
            total[:, lanes] = jnp.dot(with_ones, weight, preferred_element_type=jnp.float32)

        def one_chunk(n, unused):
            at = pl.ds(pl.multiple_of(n * CHUNK, CHUNK), CHUNK)
            key = keys[at, :]
            value = transposed(values[at, :])
            for start, width in LANES:
                lanes = pl.ds(start, width)
                score = lax.dot_general(key, query[lanes, :], nt, preferred_element_type=jnp.float32)
                before = top[:1, lanes]
                highest = jnp.maximum(before, jnp.max(score, axis=0, keepdims=True))
                weight = jnp.exp2(score * scale - highest * scale).astype(jnp.bfloat16)
                factor = jnp.exp2((before - highest) * scale)
                top[:, lanes] = jnp.broadcast_to(highest, (8, width))
                total[:, lanes] = total[:, lanes] * factor + jnp.dot(
                    value, weight, preferred_element_type=jnp.float32
                )
            return unused

        lax.fori_loop(0, (filled + CHUNK - 1) // CHUNK, one_chunk, 0)
        for h in range(GROUP):
            lanes = pl.ds(h * PAGE, PAGE)
            out_ref[h * HD : (h + 1) * HD, rows] = (total[:HD, lanes] / total[HD : HD + 1, lanes]).astype(
                jnp.bfloat16
            )
        return unused

    lax.fori_loop(0, pages_here, one_lost, 0)


def attend(queries, new_kv, kv, page_slot, parent, valid_count, lost_parent):
    rows = kv.shape[1]
    smem = pl.BlockSpec(memory_space=pltpu.SMEM)
    vmem = pl.BlockSpec(memory_space=pltpu.VMEM)
    return pl.pallas_call(
        attention_kernel,
        out_shape=jax.ShapeDtypeStruct(queries.shape[::-1], jnp.bfloat16),
        in_specs=[smem] * 4 + [vmem] * 3,
        out_specs=vmem,
        scratch_shapes=[
            pltpu.VMEM((rows + CHUNK, HD), jnp.bfloat16),
            pltpu.VMEM((rows + CHUNK, 2 * HD), jnp.bfloat16),
            pltpu.VMEM((GROUP * PAGE, HD), jnp.bfloat16),
            pltpu.VMEM((8, GROUP * PAGE), jnp.float32),
            pltpu.VMEM((HD + EXTRA, GROUP * PAGE), jnp.float32),
        ],
        compiler_params=pltpu.CompilerParams(vmem_limit_bytes=VMEM_LIMIT),
        name="attend",
    )(page_slot, parent, valid_count, lost_parent, queries, new_kv, kv)


OWN = [(0, 0), (0, 1)]
NEAR = [(1, 0), (3, 0), (1, 1), (3, 1)]
FAR = [(2, 0), (2, 1)]
WAVES = []
for _w in range(6):
    for _delay, _blocks in ((0, OWN), (1, NEAR), (2, FAR)):
        if 0 <= _w - _delay < 4:
            WAVES += [(_block, _w - _delay) for _block in _blocks]


def project_kernel(
    att_ref, w_ref, out_ref, peers, terms, outgoing, incoming, a_send, a_recv, z_send, z_recv, f_send, f_recv
):
    x, y, k, t = place()
    here = ctx_of(x, y, k)

    def holder(dy, dk):
        return (ctx_of(x, lax.rem(y + dy, 4), k if dk == 0 else 1 - k), t)

    columns = w_ref.shape[0] // 4
    width = att_ref.shape[1] // 2
    sides = (pl.ds(0, width), pl.ds(width, width))
    mine = lax.rem(y, 2) * 2 + k
    late = lax.rem(t + lax.div(y, 2), 2)
    barrier = pltpu.get_barrier_semaphore()
    others = [(dy, dk) for dy in range(4) for dk in range(2) if (dy, dk) != (0, 0)]
    for device in [holder(dy, dk) for dy, dk in others] + [(here, lax.rem(t + 1, 8)), (here, lax.rem(t + 7, 8))]:
        pl.semaphore_signal(barrier, inc=1, device_id=device, device_id_type=MESH)
    pl.semaphore_wait(barrier, 9)

    a_copies = []

    def share(src, dst, device):
        n = len(a_copies)
        copy = pltpu.make_async_remote_copy(
            src, dst, a_send.at[n], a_recv.at[n], device_id=device, device_id_type=MESH
        )
        copy.start()
        a_copies.append(copy)
        return copy

    core = {0: share(att_ref, peers.at[0, 1], holder(0, 1))}
    near = {3: share(att_ref, peers.at[3, 0], holder(1, 0)), 1: share(att_ref, peers.at[1, 0], holder(3, 0))}
    far = {}

    def need(dy, dk):
        if (dy, dk) == (0, 0):
            return
        if dk == 1:
            core[dy].wait_recv()
        elif dy in near:
            near[dy].wait_recv()
            side = 0 if dy == 3 else 1
            far[side] = share(
                peers.at[dy, 0, :, sides[side]],
                peers.at[2, 0, :, sides[side]],
                holder(1 if dy == 3 else 3, 0),
            )
            core[dy] = share(peers.at[dy, 0], peers.at[dy, 1], holder(0, 1))
        else:
            far[0].wait_recv()
            far[1].wait_recv()
            core[2] = share(peers.at[2, 0], peers.at[2, 1], holder(0, 1))

    def hop(block, i, side):
        dy, dk = block
        step = (1 - 2 * k) * (1 - 2 * dk)
        slot = i + 1 - late
        return pltpu.make_async_remote_copy(
            outgoing.at[dy, dk, i, side],
            incoming.at[dy, dk, slot, side],
            z_send.at[dy, dk, i, side],
            z_recv.at[dy, dk, slot, side],
            device_id=(here, lax.rem(t + step + 8, 8)),
            device_id_type=MESH,
        )

    def arrived(block, i, side):
        dy, dk = block
        spot = incoming.at[dy, dk, i, side]
        pltpu.make_async_copy(spot, spot, z_recv.at[dy, dk, i, side]).wait()

    spot = pl.ds(pl.multiple_of(mine * columns, 16), columns)

    def result(block, side):
        dy, dk = block
        return pltpu.make_async_remote_copy(
            outgoing.at[dy, dk, 3, side],
            out_ref.at[spot, sides[side]],
            f_send.at[dy, dk, side],
            f_recv.at[mine, side],
            device_id=holder(dy, dk),
            device_id_type=MESH,
        )

    def add(block, i, side):
        dy, dk = block
        step = (1 - 2 * k) * (1 - 2 * dk)
        target = lax.rem(t - step * (2 * i + 2 - late) + 16, 8)
        at = pl.ds(pl.multiple_of(lax.div(target, 2) * columns, 32), columns)
        return terms[dy, dk, at, side * width : (side + 1) * width]

    def first(block, i):
        dy, dk = block
        for side in (0, 1):
            outgoing[dy, dk, i, side] = add(block, i, side).astype(jnp.bfloat16)
            hop(block, i, side).start()

    def pass_on(block, i):
        dy, dk = block
        for side in (0, 1):
            arrived(block, i, side)
            total = add(block, i, side) + incoming[dy, dk, i, side].astype(jnp.float32)
            outgoing[dy, dk, i, side] = total.astype(jnp.bfloat16)
            hop(block, i, side).start()

    def finish(block, i):
        dy, dk = block
        for side in (0, 1):
            arrived(block, i, side)
            total = add(block, i, side) + incoming[dy, dk, i, side].astype(jnp.float32)
            if block == (0, 0):
                out_ref[spot, sides[side]] = total.astype(jnp.bfloat16)
            else:
                outgoing[dy, dk, i, side] = total.astype(jnp.bfloat16)
                result(block, side).start()

    for block, i in WAVES:
        dy, dk = block
        if i == 0:
            need(dy, dk)
            rows = att_ref[...] if block == (0, 0) else peers[dy, dk]
            terms[dy, dk] = jnp.dot(w_ref[...], rows, preferred_element_type=jnp.float32)
            pl.when(late == 1)(lambda block=block: first(block, 0))
            pl.when(late == 0)(lambda block=block: pass_on(block, 0))
        elif i < 3:
            pass_on(block, i)
        else:
            pl.when(late == 1)(lambda block=block: pass_on(block, 3))
            pl.when(late == 0)(lambda block=block: finish(block, 3))

    for n in range(4):

        @pl.when((late == 1) | (mine != n))
        def _(n=n):
            for side in (0, 1):
                landed = out_ref.at[pl.ds(n * columns, columns), sides[side]]
                pltpu.make_async_copy(landed, landed, f_recv.at[n, side]).wait()

    for copy in a_copies:
        copy.wait_send()
    for block in OWN + NEAR + FAR:
        for i in range(3):
            hop(block, i, 0).wait_send()
            hop(block, i, 1).wait_send()

        @pl.when(late == 1)
        def _(block=block):
            hop(block, 3, 0).wait_send()
            hop(block, 3, 1).wait_send()

        if block != (0, 0):

            @pl.when(late == 0)
            def _(block=block):
                result(block, 0).wait_send()
                result(block, 1).wait_send()


def project(attended, weights):
    depth, rows = attended.shape
    columns = weights.shape[0] // 4
    vmem = pl.BlockSpec(memory_space=pltpu.VMEM)
    return pl.pallas_call(
        project_kernel,
        out_shape=jax.ShapeDtypeStruct((4 * columns, rows), jnp.bfloat16),
        in_specs=[vmem, vmem],
        out_specs=vmem,
        scratch_shapes=[
            pltpu.VMEM((4, 2, depth, rows), jnp.bfloat16),
            pltpu.VMEM((4, 2, 4 * columns, rows), jnp.float32),
            pltpu.VMEM((4, 2, 4, 2, columns, rows // 2), jnp.bfloat16),
            pltpu.VMEM((4, 2, 4, 2, columns, rows // 2), jnp.bfloat16),
            pltpu.SemaphoreType.DMA((8,)),
            pltpu.SemaphoreType.DMA((8,)),
            pltpu.SemaphoreType.DMA((4, 2, 4, 2)),
            pltpu.SemaphoreType.DMA((4, 2, 4, 2)),
            pltpu.SemaphoreType.DMA((4, 2, 2)),
            pltpu.SemaphoreType.DMA((4, 2)),
        ],
        compiler_params=pltpu.CompilerParams(
            collective_id=1, has_side_effects=True, vmem_limit_bytes=VMEM_LIMIT
        ),
        name="project",
    )(attended, weights)


def per_device(
    queries, new_kv, page_cache, out_weight, page_slot, parent, valid_count, lost_parent
):
    kv, weights = gather_pages(page_cache, out_weight.T)
    kv = kv.reshape(2, -1, HD)
    attended = attend(queries, new_kv, kv, page_slot, parent, valid_count, lost_parent)
    return project(attended, weights.reshape(-1, weights.shape[2])).T


def solution(mesh):
    return jax.shard_map(
        per_device,
        mesh=mesh,
        in_specs=(
            P("ctx", "tp"),
            P(None, "ctx", "tp"),
            P(None, "ctx", "tp"),
            P("tp", "ctx"),
            P(),
            P(),
            P(),
            P(),
        ),
        out_specs=P("ctx", "tp"),
        check_vma=False,
    )
```

```python
import math

import jax
import jax.numpy as jnp
from jax import lax
from jax.experimental import pallas as pl
from jax.experimental.pallas import tpu as pltpu
from jax.sharding import PartitionSpec as P

HEADS = 56
KV_HEADS = 8
HD = 128
PAGE = 128
GROUP = HEADS // KV_HEADS
CHUNK = 768
MESH = pl.DeviceIdType.MESH
VMEM_LIMIT = 56 * 2**20


def place():
    c = lax.axis_index("ctx")
    return lax.div(c, 8), lax.rem(lax.div(c, 2), 4), lax.rem(c, 2), lax.axis_index("tp")


def ctx_of(x, y, k):
    return (x * 4 + y) * 2 + k


def gather_kernel(page_ref, w_ref, kv_ref, wall_ref, own_sem, send_sem, recv_sem):
    x, y, k, t = place()

    def at_x(d):
        return (ctx_of(lax.rem(x + d, 4), y, k), t)

    def at_y(d):
        return (ctx_of(x, lax.rem(y + d, 4), k), t)

    other = (ctx_of(x, y, 1 - k), t)
    barrier = pltpu.get_barrier_semaphore()
    for device in (at_x(1), at_x(2), at_x(3), at_y(1), at_y(2), at_y(3), other):
        pl.semaphore_signal(barrier, inc=1, device_id=device, device_id_type=MESH)
    own = pltpu.make_async_copy(page_ref, kv_ref.at[:, x, y, k], own_sem.at[0])
    own.start()
    kept = pltpu.make_async_copy(w_ref, wall_ref.at[x], own_sem.at[1])
    pl.when(k == 0)(kept.start)
    pl.semaphore_wait(barrier, 7)

    copies = []

    def remote(src, dst, device):
        n = len(copies)
        copy = pltpu.make_async_remote_copy(
            src, dst, send_sem.at[n], recv_sem.at[n], device_id=device, device_id_type=MESH
        )
        copy.start()
        copies.append(copy)
        return copy

    def piece(dx, dy):
        return kv_ref.at[:, lax.rem(x + dx, 4), lax.rem(y + dy, 4), k]

    def half(part, dx, dy):
        return kv_ref.at[part, lax.rem(x + dx, 4), lax.rem(y + dy, 4), k]

    swapped = pltpu.make_async_remote_copy(
        w_ref, wall_ref.at[x], own_sem.at[2], own_sem.at[3], device_id=at_y(2), device_id_type=MESH
    )
    home = piece(0, 0)
    along = {d: remote(page_ref, home, at_x(d)) for d in (1, 3, 2)}
    up = {0: remote(page_ref, home, at_y(1))}
    down = {0: remote(page_ref, home, at_y(3))}
    pl.when(k == 1)(swapped.start)
    shared = [remote(page_ref, home, other)]
    for d in (1, 3, 2):
        along[d].wait_recv()
        here = piece(4 - d, 0)
        up[d] = remote(here, here, at_y(1))
        down[d] = remote(here, here, at_y(3))
        shared.append(remote(here, here, other))
    pl.when(k == 0)(kept.wait)
    pl.when(k == 1)(swapped.wait_recv)
    right = remote(wall_ref.at[x], wall_ref.at[x], at_x(1))
    left = remote(wall_ref.at[x], wall_ref.at[x], at_x(3))
    far = {}
    far_w = []
    middle = w_ref.shape[0] // 2
    for d in (0, 1, 3, 2):
        dx = (4 - d) % 4
        up[d].wait_recv()
        here = half(0, dx, 3)
        far[0, d] = remote(here, here, at_y(1))
        shared.append(remote(piece(dx, 3), piece(dx, 3), other))
        down[d].wait_recv()
        here = half(1, dx, 1)
        far[1, d] = remote(here, here, at_y(3))
        shared.append(remote(piece(dx, 1), piece(dx, 1), other))
        if d == 3:
            right.wait_recv()
            here = wall_ref.at[lax.rem(x + 3, 4), pl.ds(0, middle)]
            far_w.append(remote(here, here, at_x(1)))
            left.wait_recv()
            here = wall_ref.at[lax.rem(x + 1, 4), pl.ds(middle, middle)]
            far_w.append(remote(here, here, at_x(3)))
    for d in (0, 1, 3, 2):
        far[0, d].wait_recv()
        far[1, d].wait_recv()
        here = piece((4 - d) % 4, 2)
        shared.append(remote(here, here, other))
    for copy in far_w:
        copy.wait_recv()
    for copy in shared:
        copy.wait_recv()
    for copy in copies:
        copy.wait_send()
    pl.when(k == 1)(swapped.wait_send)
    own.wait()


GATHER_COPIES = 6 + 9 + 2 + 16 + 2 + 4


def gather_pages(page_cache, weights):
    rows = page_cache.shape[1]
    anywhere = pl.BlockSpec(memory_space=pl.ANY)
    return pl.pallas_call(
        gather_kernel,
        out_shape=(
            jax.ShapeDtypeStruct((2, 4, 4, 2, rows, HD), jnp.bfloat16),
            jax.ShapeDtypeStruct((4,) + weights.shape, jnp.bfloat16),
        ),
        in_specs=[anywhere, anywhere],
        out_specs=(anywhere, anywhere),
        scratch_shapes=[
            pltpu.SemaphoreType.DMA((4,)),
            pltpu.SemaphoreType.DMA((GATHER_COPIES,)),
            pltpu.SemaphoreType.DMA((GATHER_COPIES,)),
        ],
        compiler_params=pltpu.CompilerParams(collective_id=0, has_side_effects=True),
        name="gather_pages",
    )(page_cache, weights)


LANES = ((0, GROUP * PAGE),)
EXTRA = 16


def attention_kernel(
    slot_ref, parent_ref, count_ref, lost_ref, q_ref, new_ref, kv_ref, out_ref, keys, values, query, top, total
):
    pages_here = q_ref.shape[0] // PAGE
    scale = math.log2(math.e) / math.sqrt(HD)
    base = lax.axis_index("ctx") * pages_here
    token = lax.broadcasted_iota(jnp.int32, (16, HD), 0)
    nt = (((1,), (1,)), ((), ()))

    def transposed(block):
        return block.T[: HD + EXTRA]

    def one_lost(j, unused):
        rows = pl.ds(pl.multiple_of(j * PAGE, PAGE), PAGE)

        def append(state):
            page, filled = state
            count = count_ref[page]
            first = slot_ref[page] * PAGE
            at = pl.ds(pl.multiple_of(first, PAGE), PAGE)
            to = pl.ds(pl.multiple_of(filled, 16), PAGE)
            keys[to, :] = kv_ref[0, at, :]
            values[to, :HD] = kv_ref[1, at, :]
            values[to, HD:] = jnp.ones((PAGE, HD), jnp.bfloat16)
            last = ((count - 1) // 16) * 16
            kept = token + last < count
            at = pl.ds(pl.multiple_of(first + last, 16), 16)
            to = pl.ds(pl.multiple_of(filled + last, 16), 16)
            lead = kv_ref[0, pl.ds(pl.multiple_of(first, PAGE), 16), :].astype(jnp.float32)[:1, :]
            keys[to, :] = jnp.where(kept, kv_ref[0, at, :].astype(jnp.float32), lead).astype(jnp.bfloat16)
            values[to, :HD] = jnp.where(kept, kv_ref[1, at, :].astype(jnp.float32), 0.0).astype(jnp.bfloat16)
            values[to, HD:] = kept.astype(jnp.float32).astype(jnp.bfloat16)
            return parent_ref[page], filled + last + 16

        unused_page, filled = lax.while_loop(
            lambda state: state[0] >= 0, append, (lost_ref[base + j], jnp.int32(0))
        )
        tail = pl.ds(pl.multiple_of(filled, 16), CHUNK)
        lead = keys[:16, :].astype(jnp.float32)[:1, :]
        keys[tail, :] = jnp.broadcast_to(lead, (CHUNK, HD)).astype(jnp.bfloat16)
        values[tail, :] = jnp.zeros((CHUNK, 2 * HD), jnp.bfloat16)
        for h in range(GROUP):
            query[h * PAGE : (h + 1) * PAGE, :] = q_ref[rows, h * HD : (h + 1) * HD]

        with_ones = transposed(
            jnp.concatenate([new_ref[1, rows, :], jnp.ones((PAGE, HD), jnp.bfloat16)], axis=1)
        )
        for start, width in LANES:
            lanes = pl.ds(start, width)
            score = lax.dot_general(
                new_ref[0, rows, :], query[lanes, :], nt, preferred_element_type=jnp.float32
            )
            k_at = lax.broadcasted_iota(jnp.int32, (PAGE, width), 0)
            q_at = lax.broadcasted_iota(jnp.int32, (PAGE, width), 1) % PAGE
            seen = k_at <= q_at
            score = jnp.where(seen, score, -1e30)
            highest = jnp.max(score, axis=0, keepdims=True)
            weight = jnp.where(seen, jnp.exp2(score * scale - highest * scale), 0.0).astype(jnp.bfloat16)
            top[:, lanes] = jnp.broadcast_to(highest, (8, width))
            total[:, lanes] = jnp.dot(with_ones, weight, preferred_element_type=jnp.float32)

        def one_chunk(n, unused):
            at = pl.ds(pl.multiple_of(n * CHUNK, CHUNK), CHUNK)
            key = keys[at, :]
            value = transposed(values[at, :])
            for start, width in LANES:
                lanes = pl.ds(start, width)
                score = lax.dot_general(key, query[lanes, :], nt, preferred_element_type=jnp.float32)
                before = top[:1, lanes]
                highest = jnp.maximum(before, jnp.max(score, axis=0, keepdims=True))
                weight = jnp.exp2(score * scale - highest * scale).astype(jnp.bfloat16)
                factor = jnp.exp2((before - highest) * scale)
                top[:, lanes] = jnp.broadcast_to(highest, (8, width))
                total[:, lanes] = total[:, lanes] * factor + jnp.dot(
                    value, weight, preferred_element_type=jnp.float32
                )
            return unused

        lax.fori_loop(0, (filled + CHUNK - 1) // CHUNK, one_chunk, 0)
        for h in range(GROUP):
            lanes = pl.ds(h * PAGE, PAGE)
            out_ref[h * HD : (h + 1) * HD, rows] = (total[:HD, lanes] / total[HD : HD + 1, lanes]).astype(
                jnp.bfloat16
            )
        return unused

    lax.fori_loop(0, pages_here, one_lost, 0)


def attend(queries, new_kv, kv, page_slot, parent, valid_count, lost_parent):
    rows = kv.shape[1]
    smem = pl.BlockSpec(memory_space=pltpu.SMEM)
    vmem = pl.BlockSpec(memory_space=pltpu.VMEM)
    return pl.pallas_call(
        attention_kernel,
        out_shape=jax.ShapeDtypeStruct(queries.shape[::-1], jnp.bfloat16),
        in_specs=[smem] * 4 + [vmem] * 3,
        out_specs=vmem,
        scratch_shapes=[
            pltpu.VMEM((rows + CHUNK, HD), jnp.bfloat16),
            pltpu.VMEM((rows + CHUNK, 2 * HD), jnp.bfloat16),
            pltpu.VMEM((GROUP * PAGE, HD), jnp.bfloat16),
            pltpu.VMEM((8, GROUP * PAGE), jnp.float32),
            pltpu.VMEM((HD + EXTRA, GROUP * PAGE), jnp.float32),
        ],
        compiler_params=pltpu.CompilerParams(vmem_limit_bytes=VMEM_LIMIT),
        name="attend",
    )(page_slot, parent, valid_count, lost_parent, queries, new_kv, kv)


PARTS = [((0, 0), (0, 1), 0), ((0, 1), (0, 1), 0)]
PARTS += [((dy, dk), (0,), 2) for dy in (1, 3) for dk in (0, 1)]
PARTS += [((dy, dk), (1,), 3) for dy in (1, 3) for dk in (0, 1)]
PARTS += [((2, dk), (0,), 3) for dk in (0, 1)]
PARTS += [((2, dk), (1,), 4) for dk in (0, 1)]
STEPS = 5
WAVES = [
    (block, sides, wave - delay)
    for wave in range(STEPS + 4)
    for block, sides, delay in PARTS
    if 0 <= wave - delay < STEPS
]
EVEN = ((4, None, 0), (-2, 2, 2), (2, 0, 1))
ODD = ((-3, None, 2), (3, 0, 0), (-1, 2, 3), (1, 1, 1))


def project_kernel(
    att_ref, w_ref, out_ref, peers, terms, outgoing, incoming, a_send, a_recv, z_send, z_recv, f_send, f_recv
):
    x, y, k, t = place()
    here = ctx_of(x, y, k)

    def holder(dy, dk):
        return (ctx_of(x, lax.rem(y + dy, 4), k if dk == 0 else 1 - k), t)

    columns = w_ref.shape[0] // 4
    width = att_ref.shape[1] // 2
    lanes = (pl.ds(0, width), pl.ds(width, width))
    mine = lax.rem(y, 2) * 2 + k
    odd = lax.rem(t + lax.div(y, 2) + k, 2)
    barrier = pltpu.get_barrier_semaphore()
    others = [(dy, dk) for dy in range(4) for dk in range(2) if (dy, dk) != (0, 0)]
    for device in [holder(dy, dk) for dy, dk in others] + [(here, lax.rem(t + 1, 8)), (here, lax.rem(t + 7, 8))]:
        pl.semaphore_signal(barrier, inc=1, device_id=device, device_id_type=MESH)
    pl.semaphore_wait(barrier, 9)

    def share(src, dy, dk, side, device):
        copy = pltpu.make_async_remote_copy(
            src,
            peers.at[dy, dk, side],
            a_send.at[dy, dk, side],
            a_recv.at[dy, dk, side],
            device_id=device,
            device_id_type=MESH,
        )
        copy.start()
        return copy

    shared = {}
    for side in (0, 1):
        mine_here = att_ref.at[:, lanes[side]]
        shared[3, 0, side] = share(mine_here, 3, 0, side, holder(1, 0))
        shared[1, 0, side] = share(mine_here, 1, 0, side, holder(3, 0))
        shared[0, 1, side] = share(mine_here, 0, 1, side, holder(0, 1))

    def need(dy, dk, side):
        if (dy, dk) == (0, 0):
            return
        shared[dy, dk, side].wait_recv()
        if dk == 0:
            if dy == (3 if side == 0 else 1):
                shared[2, 0, side] = share(peers.at[dy, 0, side], 2, 0, side, holder(4 - dy, 0))
            shared[dy, 1, side] = share(peers.at[dy, 0, side], dy, 1, side, holder(0, 1))

    def long_way(dk):
        return (1 - 2 * k) * (1 - 2 * dk)

    def hop(block, i, side, arm, slot):
        dy, dk = block
        step = long_way(dk) if arm > 0 else -long_way(dk)
        return pltpu.make_async_remote_copy(
            outgoing.at[dy, dk, i, side],
            incoming.at[dy, dk, slot, side],
            z_send.at[dy, dk, i, side],
            z_recv.at[dy, dk, slot, side],
            device_id=(here, lax.rem(t + step + 8, 8)),
            device_id_type=MESH,
        )

    def arrived(block, slot, side):
        dy, dk = block
        spot = incoming.at[dy, dk, slot, side]
        pltpu.make_async_copy(spot, spot, z_recv.at[dy, dk, slot, side]).wait()
        return incoming[dy, dk, slot, side].astype(jnp.float32)

    spot = pl.ds(pl.multiple_of(mine * columns, 16), columns)

    def result(block, side):
        dy, dk = block
        return pltpu.make_async_remote_copy(
            outgoing.at[dy, dk, 3, side],
            out_ref.at[spot, lanes[side]],
            f_send.at[dy, dk, side],
            f_recv.at[mine, side],
            device_id=holder(dy, dk),
            device_id_type=MESH,
        )

    def term(block, distance, side):
        dy, dk = block
        target = lax.rem(t + long_way(dk) * distance + 8, 8)
        at = pl.ds(pl.multiple_of(lax.div(target, 2) * columns, 32), columns)
        return terms[dy, dk, at, side * width : (side + 1) * width]

    def pass_on(block, sides, i, table):
        dy, dk = block
        distance, source, slot = table[i]
        for side in sides:
            total = term(block, distance, side)
            if source is not None:
                total = total + arrived(block, source, side)
            outgoing[dy, dk, i, side] = total.astype(jnp.bfloat16)
            hop(block, i, side, distance, slot).start()

    def finish(block, sides):
        dy, dk = block
        for side in sides:
            total = term(block, 0, side) + arrived(block, 3, side) + arrived(block, 1, side)
            if block == (0, 0):
                out_ref[spot, lanes[side]] = total.astype(jnp.bfloat16)
            else:
                outgoing[dy, dk, 3, side] = total.astype(jnp.bfloat16)
                result(block, side).start()

    for block, sides, i in WAVES:
        dy, dk = block
        if i == 0:
            for side in sides:
                need(dy, dk, side)
            if block == (0, 0):
                rows = att_ref[...]
            elif len(sides) == 2:
                rows = jnp.concatenate([peers[dy, dk, 0], peers[dy, dk, 1]], axis=1)
            else:
                rows = peers[dy, dk, sides[0]]
            start = sides[0] * width
            terms[dy, dk, :, start : start + len(sides) * width] = jnp.dot(
                w_ref[...], rows, preferred_element_type=jnp.float32
            )
        if i < 4:
            pl.when(odd == 1)(lambda block=block, sides=sides, i=i: pass_on(block, sides, i, ODD))
        if i < 3:
            pl.when(odd == 0)(lambda block=block, sides=sides, i=i: pass_on(block, sides, i, EVEN))
        if i == 4:
            pl.when(odd == 0)(lambda block=block, sides=sides: finish(block, sides))

    for n in range(4):

        @pl.when((odd == 1) | (mine != n))
        def _(n=n):
            for side in (0, 1):
                landed = out_ref.at[pl.ds(n * columns, columns), lanes[side]]
                pltpu.make_async_copy(landed, landed, f_recv.at[n, side]).wait()

    for copy in shared.values():
        copy.wait_send()

    def drain(block, table):
        for i, (distance, source, slot) in enumerate(table):
            for side in (0, 1):
                hop(block, i, side, distance, slot).wait_send()

    for block in [(0, 0)] + others:
        pl.when(odd == 1)(lambda block=block: drain(block, ODD))

        @pl.when(odd == 0)
        def _(block=block):
            drain(block, EVEN)
            if block != (0, 0):
                result(block, 0).wait_send()
                result(block, 1).wait_send()


def project(attended, weights):
    depth, rows = attended.shape
    columns = weights.shape[0] // 4
    vmem = pl.BlockSpec(memory_space=pltpu.VMEM)
    return pl.pallas_call(
        project_kernel,
        out_shape=jax.ShapeDtypeStruct((4 * columns, rows), jnp.bfloat16),
        in_specs=[vmem, vmem],
        out_specs=vmem,
        scratch_shapes=[
            pltpu.VMEM((4, 2, 2, depth, rows // 2), jnp.bfloat16),
            pltpu.VMEM((4, 2, 4 * columns, rows), jnp.float32),
            pltpu.VMEM((4, 2, 4, 2, columns, rows // 2), jnp.bfloat16),
            pltpu.VMEM((4, 2, 4, 2, columns, rows // 2), jnp.bfloat16),
            pltpu.SemaphoreType.DMA((4, 2, 2)),
            pltpu.SemaphoreType.DMA((4, 2, 2)),
            pltpu.SemaphoreType.DMA((4, 2, 4, 2)),
            pltpu.SemaphoreType.DMA((4, 2, 4, 2)),
            pltpu.SemaphoreType.DMA((4, 2, 2)),
            pltpu.SemaphoreType.DMA((4, 2)),
        ],
        compiler_params=pltpu.CompilerParams(
            collective_id=1, has_side_effects=True, vmem_limit_bytes=VMEM_LIMIT
        ),
        name="project",
    )(attended, weights)


def per_device(
    queries, new_kv, page_cache, out_weight, page_slot, parent, valid_count, lost_parent
):
    kv, weights = gather_pages(page_cache, out_weight.T)
    kv = kv.reshape(2, -1, HD)
    attended = attend(queries, new_kv, kv, page_slot, parent, valid_count, lost_parent)
    return project(attended, weights.reshape(-1, weights.shape[2])).T


def solution(mesh):
    return jax.shard_map(
        per_device,
        mesh=mesh,
        in_specs=(
            P("ctx", "tp"),
            P(None, "ctx", "tp"),
            P(None, "ctx", "tp"),
            P("tp", "ctx"),
            P(),
            P(),
            P(),
            P(),
        ),
        out_specs=P("ctx", "tp"),
        check_vma=False,
    )
```

```python
import math

import jax
import jax.numpy as jnp
from jax import lax
from jax.experimental import pallas as pl
from jax.experimental.pallas import tpu as pltpu
from jax.sharding import PartitionSpec as P

HEADS = 56
KV_HEADS = 8
HD = 128
PAGE = 128
GROUP = HEADS // KV_HEADS
CHUNK = 512
MESH = pl.DeviceIdType.MESH
VMEM_LIMIT = 56 * 2**20


def place():
    c = lax.axis_index("ctx")
    return lax.div(c, 8), lax.rem(lax.div(c, 2), 4), lax.rem(c, 2), lax.axis_index("tp")


def ctx_of(x, y, k):
    return (x * 4 + y) * 2 + k


def gather_kernel(page_ref, w_ref, kv_ref, wall_ref, own_sem, send_sem, recv_sem):
    x, y, k, t = place()

    def at_x(d):
        return (ctx_of(lax.rem(x + d, 4), y, k), t)

    def at_y(d):
        return (ctx_of(x, lax.rem(y + d, 4), k), t)

    other = (ctx_of(x, y, 1 - k), t)
    barrier = pltpu.get_barrier_semaphore()
    for device in (at_x(1), at_x(2), at_x(3), at_y(1), at_y(2), at_y(3), other):
        pl.semaphore_signal(barrier, inc=1, device_id=device, device_id_type=MESH)
    own = pltpu.make_async_copy(page_ref, kv_ref.at[:, x, y, k], own_sem.at[0])
    own.start()
    kept = pltpu.make_async_copy(w_ref, wall_ref.at[x], own_sem.at[1])
    pl.when(k == 0)(kept.start)
    pl.semaphore_wait(barrier, 7)

    copies = []

    def remote(src, dst, device, odd_src=None):
        n = len(copies)

        def copy_from(ref):
            return pltpu.make_async_remote_copy(
                ref, dst, send_sem.at[n], recv_sem.at[n], device_id=device, device_id_type=MESH
            )

        copy = copy_from(src)
        if odd_src is None:
            copy.start()
        else:
            pl.when(k == 0)(copy.start)
            pl.when(k == 1)(copy_from(odd_src).start)
        copies.append(copy)
        return copy

    def piece(dx, dy):
        return kv_ref.at[:, lax.rem(x + dx, 4), lax.rem(y + dy, 4), k]

    def half(part, dx, dy):
        return kv_ref.at[part, lax.rem(x + dx, 4), lax.rem(y + dy, 4), k]

    middle = w_ref.shape[0] // 2
    halves = (pl.ds(0, middle), pl.ds(middle, middle))
    swapped = [
        pltpu.make_async_remote_copy(
            w_ref.at[halves[n]],
            wall_ref.at[x, halves[n]],
            own_sem.at[2 + n],
            own_sem.at[4 + n],
            device_id=(ctx_of(x, 3 - y, k), t),
            device_id_type=MESH,
        )
        for n in (0, 1)
    ]
    for copy in swapped:
        pl.when(k == 1)(copy.start)
    home = piece(0, 0)
    along = {d: remote(page_ref, home, at_x(d)) for d in (1, 3, 2)}
    up = {0: remote(page_ref, home, at_y(1))}
    down = {0: remote(page_ref, home, at_y(3))}
    shared = [remote(page_ref, home, other)]
    for d in (1, 3, 2):
        along[d].wait_recv()
        here = piece(4 - d, 0)
        up[d] = remote(here, here, at_y(1))
        down[d] = remote(here, here, at_y(3))
        shared.append(remote(here, here, other))
    for copy in swapped:
        pl.when(k == 1)(copy.wait_recv)
    right = {}
    left = {}
    for n in (0, 1):
        here = wall_ref.at[x, halves[n]]
        right[n] = remote(w_ref.at[halves[n]], here, at_x(1), here)
        here = wall_ref.at[x, halves[1 - n]]
        left[1 - n] = remote(w_ref.at[halves[1 - n]], here, at_x(3), here)
    far = {}
    far_w = []
    for d in (0, 1, 3, 2):
        dx = (4 - d) % 4
        up[d].wait_recv()
        here = half(0, dx, 3)
        far[0, d] = remote(here, here, at_y(1))
        shared.append(remote(piece(dx, 3), piece(dx, 3), other))
        down[d].wait_recv()
        here = half(1, dx, 1)
        far[1, d] = remote(here, here, at_y(3))
        shared.append(remote(piece(dx, 1), piece(dx, 1), other))
        if d == 3:
            right[0].wait_recv()
            here = wall_ref.at[lax.rem(x + 3, 4), halves[0]]
            far_w.append(remote(here, here, at_x(1)))
            left[1].wait_recv()
            here = wall_ref.at[lax.rem(x + 1, 4), halves[1]]
            far_w.append(remote(here, here, at_x(3)))
            far_w += [right[1], left[0]]
    for d in (0, 1, 3, 2):
        far[0, d].wait_recv()
        far[1, d].wait_recv()
        here = piece((4 - d) % 4, 2)
        shared.append(remote(here, here, other))
    for copy in far_w:
        copy.wait_recv()
    for copy in shared:
        copy.wait_recv()
    for copy in copies:
        copy.wait_send()
    for copy in swapped:
        pl.when(k == 1)(copy.wait_send)
    pl.when(k == 0)(kept.wait)
    own.wait()


GATHER_COPIES = 6 + 9 + 4 + 16 + 2 + 4


def gather_pages(page_cache, weights):
    rows = page_cache.shape[1]
    anywhere = pl.BlockSpec(memory_space=pl.ANY)
    return pl.pallas_call(
        gather_kernel,
        out_shape=(
            jax.ShapeDtypeStruct((2, 4, 4, 2, rows, HD), jnp.bfloat16),
            jax.ShapeDtypeStruct((4,) + weights.shape, jnp.bfloat16),
        ),
        in_specs=[anywhere, anywhere],
        out_specs=(anywhere, anywhere),
        scratch_shapes=[
            pltpu.SemaphoreType.DMA((6,)),
            pltpu.SemaphoreType.DMA((GATHER_COPIES,)),
            pltpu.SemaphoreType.DMA((GATHER_COPIES,)),
        ],
        compiler_params=pltpu.CompilerParams(collective_id=0, has_side_effects=True),
        name="gather_pages",
    )(page_cache, weights)


LANES = ((0, GROUP * PAGE),)
EXTRA = 16


def attention_kernel(
    slot_ref, parent_ref, count_ref, lost_ref, q_ref, new_ref, kv_ref, out_ref, keys, values, query, top, total,
    score_a, score_b, peak_a, peak_b
):
    pages_here = q_ref.shape[0] // PAGE
    scale = math.log2(math.e) / math.sqrt(HD)
    base = lax.axis_index("ctx") * pages_here
    token = lax.broadcasted_iota(jnp.int32, (16, HD), 0)
    nt = (((1,), (1,)), ((), ()))

    def transposed(block):
        return block.T[: HD + EXTRA]

    def one_lost(j, unused):
        rows = pl.ds(pl.multiple_of(j * PAGE, PAGE), PAGE)

        def append(state):
            page, filled = state
            count = count_ref[page]
            first = slot_ref[page] * PAGE
            at = pl.ds(pl.multiple_of(first, PAGE), PAGE)
            to = pl.ds(pl.multiple_of(filled, 16), PAGE)
            keys[to, :] = kv_ref[0, at, :]
            values[to, :HD] = kv_ref[1, at, :]
            values[to, HD:] = jnp.ones((PAGE, HD), jnp.bfloat16)
            last = ((count - 1) // 16) * 16
            kept = token + last < count
            at = pl.ds(pl.multiple_of(first + last, 16), 16)
            to = pl.ds(pl.multiple_of(filled + last, 16), 16)
            lead = kv_ref[0, pl.ds(pl.multiple_of(first, PAGE), 16), :].astype(jnp.float32)[:1, :]
            keys[to, :] = jnp.where(kept, kv_ref[0, at, :].astype(jnp.float32), lead).astype(jnp.bfloat16)
            values[to, :HD] = jnp.where(kept, kv_ref[1, at, :].astype(jnp.float32), 0.0).astype(jnp.bfloat16)
            values[to, HD:] = kept.astype(jnp.float32).astype(jnp.bfloat16)
            return parent_ref[page], filled + last + 16

        unused_page, filled = lax.while_loop(
            lambda state: state[0] >= 0, append, (lost_ref[base + j], jnp.int32(0))
        )
        tail = pl.ds(pl.multiple_of(filled, 16), CHUNK)
        lead = keys[:16, :].astype(jnp.float32)[:1, :]
        keys[tail, :] = jnp.broadcast_to(lead, (CHUNK, HD)).astype(jnp.bfloat16)
        values[tail, :] = jnp.zeros((CHUNK, 2 * HD), jnp.bfloat16)
        for h in range(GROUP):
            query[h * PAGE : (h + 1) * PAGE, :] = q_ref[rows, h * HD : (h + 1) * HD]

        with_ones = transposed(
            jnp.concatenate([new_ref[1, rows, :], jnp.ones((PAGE, HD), jnp.bfloat16)], axis=1)
        )
        for start, width in LANES:
            lanes = pl.ds(start, width)
            score = lax.dot_general(
                new_ref[0, rows, :], query[lanes, :], nt, preferred_element_type=jnp.float32
            )
            k_at = lax.broadcasted_iota(jnp.int32, (PAGE, width), 0)
            q_at = lax.broadcasted_iota(jnp.int32, (PAGE, width), 1) % PAGE
            seen = k_at <= q_at
            score = jnp.where(seen, score, -1e30)
            highest = jnp.max(score, axis=0, keepdims=True)
            weight = jnp.where(seen, jnp.exp2(score * scale - highest * scale), 0.0).astype(jnp.bfloat16)
            top[:, lanes] = jnp.broadcast_to(highest, (8, width))
            total[:, lanes] = jnp.dot(with_ones, weight, preferred_element_type=jnp.float32)

        def look(n, score_ref, peak_ref):
            at = pl.ds(pl.multiple_of(n * CHUNK, CHUNK), CHUNK)
            score = lax.dot_general(keys[at, :], query[...], nt, preferred_element_type=jnp.float32)
            score_ref[...] = score
            peak_ref[...] = jnp.broadcast_to(jnp.max(score, axis=0, keepdims=True), peak_ref.shape)

        def take(n, score_ref, peak_ref):
            at = pl.ds(pl.multiple_of(n * CHUNK, CHUNK), CHUNK)
            before = top[:1, :]
            highest = jnp.maximum(before, peak_ref[:1, :])
            weight = jnp.exp2(score_ref[...] * scale - highest * scale).astype(jnp.bfloat16)
            factor = jnp.exp2((before - highest) * scale)
            top[...] = jnp.broadcast_to(highest, top.shape)
            total[...] = total[...] * factor + jnp.dot(
                transposed(values[at, :]), weight, preferred_element_type=jnp.float32
            )

        def two_chunks(n, unused):
            look(2 * n + 1, score_b, peak_b)
            take(2 * n, score_a, peak_a)
            look(2 * n + 2, score_a, peak_a)
            take(2 * n + 1, score_b, peak_b)
            return unused

        chunks = (filled + CHUNK - 1) // CHUNK
        look(0, score_a, peak_a)
        lax.fori_loop(0, chunks // 2, two_chunks, 0)
        pl.when(chunks % 2 == 1)(lambda: take(chunks - 1, score_a, peak_a))
        for h in range(GROUP):
            lanes = pl.ds(h * PAGE, PAGE)
            out_ref[h * HD : (h + 1) * HD, rows] = (total[:HD, lanes] / total[HD : HD + 1, lanes]).astype(
                jnp.bfloat16
            )
        return unused

    lax.fori_loop(0, pages_here, one_lost, 0)


def attend(queries, new_kv, kv, page_slot, parent, valid_count, lost_parent):
    rows = kv.shape[1]
    smem = pl.BlockSpec(memory_space=pltpu.SMEM)
    vmem = pl.BlockSpec(memory_space=pltpu.VMEM)
    return pl.pallas_call(
        attention_kernel,
        out_shape=jax.ShapeDtypeStruct(queries.shape[::-1], jnp.bfloat16),
        in_specs=[smem] * 4 + [vmem] * 3,
        out_specs=vmem,
        scratch_shapes=[
            pltpu.VMEM((rows + 2 * CHUNK, HD), jnp.bfloat16),
            pltpu.VMEM((rows + CHUNK, 2 * HD), jnp.bfloat16),
            pltpu.VMEM((GROUP * PAGE, HD), jnp.bfloat16),
            pltpu.VMEM((8, GROUP * PAGE), jnp.float32),
            pltpu.VMEM((HD + EXTRA, GROUP * PAGE), jnp.float32),
            pltpu.VMEM((CHUNK, GROUP * PAGE), jnp.float32),
            pltpu.VMEM((CHUNK, GROUP * PAGE), jnp.float32),
            pltpu.VMEM((8, GROUP * PAGE), jnp.float32),
            pltpu.VMEM((8, GROUP * PAGE), jnp.float32),
        ],
        compiler_params=pltpu.CompilerParams(vmem_limit_bytes=VMEM_LIMIT),
        name="attend",
    )(page_slot, parent, valid_count, lost_parent, queries, new_kv, kv)


GROUPS = [
    (((0, 0, 0), (0, 0, 1)), 0.0),
    (((0, 1, 0), (0, 1, 1)), 0.4),
    (((1, 0, 0), (3, 0, 0)), 1.3),
    (((1, 1, 0), (3, 1, 0)), 1.8),
    (((1, 0, 1), (3, 0, 1)), 2.3),
    (((1, 1, 1), (3, 1, 1)), 2.7),
    (((2, 0, 0), (2, 1, 0)), 2.9),
    (((2, 0, 1), (2, 1, 1)), 3.5),
]
STEPS = 5
EVENTS = [(start - 0.05, parts, None) for parts, start in GROUPS]
EVENTS += [(start + step, parts, step) for parts, start in GROUPS for step in range(STEPS)]
EVENTS.sort(key=lambda event: event[0])
EVEN = ((4, None, 0), (-2, 2, 2), (2, 0, 1))
ODD = ((-3, None, 2), (3, 0, 0), (-1, 2, 3), (1, 1, 1))


def project_kernel(
    att_ref, w_ref, out_ref, peers, terms, outgoing, incoming, a_send, a_recv, z_send, z_recv, f_send, f_recv
):
    x, y, k, t = place()
    here = ctx_of(x, y, k)

    def holder(dy, dk):
        return (ctx_of(x, lax.rem(y + dy, 4), k if dk == 0 else 1 - k), t)

    columns = w_ref.shape[0] // 4
    width = att_ref.shape[1] // 2
    lanes = (pl.ds(0, width), pl.ds(width, width))
    mine = lax.rem(y + k, 2) * 2 + k
    odd = lax.rem(t + lax.div(y, 2) + k, 2)
    barrier = pltpu.get_barrier_semaphore()
    others = [(dy, dk) for dy in range(4) for dk in range(2) if (dy, dk) != (0, 0)]
    for device in [holder(dy, dk) for dy, dk in others] + [(here, lax.rem(t + 1, 8)), (here, lax.rem(t + 7, 8))]:
        pl.semaphore_signal(barrier, inc=1, device_id=device, device_id_type=MESH)
    pl.semaphore_wait(barrier, 9)

    def share(src, dy, dk, side, device):
        copy = pltpu.make_async_remote_copy(
            src,
            peers.at[dy, dk, side],
            a_send.at[dy, dk, side],
            a_recv.at[dy, dk, side],
            device_id=device,
            device_id_type=MESH,
        )
        copy.start()
        return copy

    shared = {}

    def share_near(side):
        mine_here = att_ref.at[:, lanes[side]]
        shared[3, 0, side] = share(mine_here, 3, 0, side, holder(1, 0))
        shared[1, 0, side] = share(mine_here, 1, 0, side, holder(3, 0))

    share_near(0)
    for side in (0, 1):
        shared[0, 1, side] = share(att_ref.at[:, lanes[side]], 0, 1, side, holder(0, 1))

    def need(dy, dk, side):
        if (dy, dk) == (0, 0):
            return
        shared[dy, dk, side].wait_recv()
        if dk == 0:
            if dy == (3 if side == 0 else 1):
                shared[2, 0, side] = share(peers.at[dy, 0, side], 2, 0, side, holder(4 - dy, 0))
            shared[dy, 1, side] = share(peers.at[dy, 0, side], dy, 1, side, holder(0, 1))

    def long_way(dk):
        return (1 - 2 * k) * (1 - 2 * dk)

    def hop(part, i, arm, slot):
        dy, dk, side = part
        step = long_way(dk) if arm > 0 else -long_way(dk)
        return pltpu.make_async_remote_copy(
            outgoing.at[dy, dk, i, side],
            incoming.at[dy, dk, slot, side],
            z_send.at[dy, dk, i, side],
            z_recv.at[dy, dk, slot, side],
            device_id=(here, lax.rem(t + step + 8, 8)),
            device_id_type=MESH,
        )

    def arrived(part, slot):
        dy, dk, side = part
        spot = incoming.at[dy, dk, slot, side]
        pltpu.make_async_copy(spot, spot, z_recv.at[dy, dk, slot, side]).wait()
        return incoming[dy, dk, slot, side].astype(jnp.float32)

    spot = pl.ds(pl.multiple_of(mine * columns, 16), columns)

    def result(part):
        dy, dk, side = part
        return pltpu.make_async_remote_copy(
            outgoing.at[dy, dk, 3, side],
            out_ref.at[spot, lanes[side]],
            f_send.at[dy, dk, side],
            f_recv.at[mine, side],
            device_id=holder(dy, dk),
            device_id_type=MESH,
        )

    def term(part, distance):
        dy, dk, side = part
        target = lax.rem(t + long_way(dk) * distance + 8, 8)
        at = pl.ds(pl.multiple_of(lax.div(target, 2) * columns, 32), columns)
        return terms[dy, dk, side, at, :]

    def pass_on(parts, i, table):
        distance, source, slot = table[i]
        for part in parts:
            dy, dk, side = part
            total = term(part, distance)
            if source is not None:
                total = total + arrived(part, source)
            outgoing[dy, dk, i, side] = total.astype(jnp.bfloat16)
            hop(part, i, distance, slot).start()

    def finish(parts):
        for part in parts:
            dy, dk, side = part
            total = term(part, 0) + arrived(part, 3) + arrived(part, 1)
            if (dy, dk) == (0, 0):
                out_ref[spot, lanes[side]] = total.astype(jnp.bfloat16)
            else:
                outgoing[dy, dk, 3, side] = total.astype(jnp.bfloat16)
                result(part).start()

    def multiply(parts):
        for part in parts:
            need(*part)
        if parts[0][:2] == (0, 0):
            rows = att_ref[...]
        else:
            rows = jnp.concatenate([peers[part] for part in parts], axis=1)
        products = jnp.dot(w_ref[...], rows, preferred_element_type=jnp.float32)
        for n, (dy, dk, side) in enumerate(parts):
            terms[dy, dk, side] = products[:, n * width : (n + 1) * width]

    for unused_time, parts, i in EVENTS:
        if i is None:
            if parts[0][0] == 1 and (1, 0, 1) not in shared:
                share_near(1)
            multiply(parts)
            continue
        if i < 4:
            pl.when(odd == 1)(lambda parts=parts, i=i: pass_on(parts, i, ODD))
        if i < 3:
            pl.when(odd == 0)(lambda parts=parts, i=i: pass_on(parts, i, EVEN))
        if i == 4:
            pl.when(odd == 0)(lambda parts=parts: finish(parts))

    for n in range(4):

        @pl.when((odd == 1) | (mine != n))
        def _(n=n):
            for side in (0, 1):
                landed = out_ref.at[pl.ds(n * columns, columns), lanes[side]]
                pltpu.make_async_copy(landed, landed, f_recv.at[n, side]).wait()

    for copy in shared.values():
        copy.wait_send()

    def drain(part, table):
        for i, (distance, source, slot) in enumerate(table):
            hop(part, i, distance, slot).wait_send()

    for parts, unused_start in GROUPS:
        for part in parts:
            pl.when(odd == 1)(lambda part=part: drain(part, ODD))

            @pl.when(odd == 0)
            def _(part=part):
                drain(part, EVEN)
                if part[:2] != (0, 0):
                    result(part).wait_send()


def project(attended, weights):
    depth, rows = attended.shape
    columns = weights.shape[0] // 4
    vmem = pl.BlockSpec(memory_space=pltpu.VMEM)
    return pl.pallas_call(
        project_kernel,
        out_shape=jax.ShapeDtypeStruct((4 * columns, rows), jnp.bfloat16),
        in_specs=[vmem, vmem],
        out_specs=vmem,
        scratch_shapes=[
            pltpu.VMEM((4, 2, 2, depth, rows // 2), jnp.bfloat16),
            pltpu.VMEM((4, 2, 2, 4 * columns, rows // 2), jnp.float32),
            pltpu.VMEM((4, 2, 4, 2, columns, rows // 2), jnp.bfloat16),
            pltpu.VMEM((4, 2, 4, 2, columns, rows // 2), jnp.bfloat16),
            pltpu.SemaphoreType.DMA((4, 2, 2)),
            pltpu.SemaphoreType.DMA((4, 2, 2)),
            pltpu.SemaphoreType.DMA((4, 2, 4, 2)),
            pltpu.SemaphoreType.DMA((4, 2, 4, 2)),
            pltpu.SemaphoreType.DMA((4, 2, 2)),
            pltpu.SemaphoreType.DMA((4, 2)),
        ],
        compiler_params=pltpu.CompilerParams(
            collective_id=1, has_side_effects=True, vmem_limit_bytes=VMEM_LIMIT
        ),
        name="project",
    )(attended, weights)


def per_device(
    queries, new_kv, page_cache, out_weight, page_slot, parent, valid_count, lost_parent
):
    kv, weights = gather_pages(page_cache, out_weight.T)
    kv = kv.reshape(2, -1, HD)
    attended = attend(queries, new_kv, kv, page_slot, parent, valid_count, lost_parent)
    return project(attended, weights.reshape(-1, weights.shape[2])).T


def solution(mesh):
    return jax.shard_map(
        per_device,
        mesh=mesh,
        in_specs=(
            P("ctx", "tp"),
            P(None, "ctx", "tp"),
            P(None, "ctx", "tp"),
            P("tp", "ctx"),
            P(),
            P(),
            P(),
            P(),
        ),
        out_specs=P("ctx", "tp"),
        check_vma=False,
    )
```

```python
import math

import jax
import jax.numpy as jnp
from jax import lax
from jax.experimental import pallas as pl
from jax.experimental.pallas import tpu as pltpu
from jax.sharding import PartitionSpec as P

HEADS = 56
KV_HEADS = 8
HD = 128
PAGE = 128
GROUP = HEADS // KV_HEADS
CHUNK = 512
MESH = pl.DeviceIdType.MESH
VMEM_LIMIT = 56 * 2**20


def place():
    c = lax.axis_index("ctx")
    return lax.div(c, 8), lax.rem(lax.div(c, 2), 4), lax.rem(c, 2), lax.axis_index("tp")


def ctx_of(x, y, k):
    return (x * 4 + y) * 2 + k


def gather_kernel(page_ref, w_ref, kv_ref, wall_ref, own_sem, send_sem, recv_sem):
    x, y, k, t = place()

    def at_x(d):
        return (ctx_of(lax.rem(x + d, 4), y, k), t)

    def at_y(d):
        return (ctx_of(x, lax.rem(y + d, 4), k), t)

    other = (ctx_of(x, y, 1 - k), t)
    barrier = pltpu.get_barrier_semaphore()
    for device in (at_x(1), at_x(2), at_x(3), at_y(1), at_y(2), at_y(3), other):
        pl.semaphore_signal(barrier, inc=1, device_id=device, device_id_type=MESH)
    own = pltpu.make_async_copy(page_ref, kv_ref.at[:, x, y, k], own_sem.at[0])
    own.start()
    kept = pltpu.make_async_copy(w_ref, wall_ref.at[x], own_sem.at[1])
    pl.when(k == 0)(kept.start)
    pl.semaphore_wait(barrier, 7)

    copies = []

    def remote(src, dst, device, odd_src=None):
        n = len(copies)

        def copy_from(ref):
            return pltpu.make_async_remote_copy(
                ref, dst, send_sem.at[n], recv_sem.at[n], device_id=device, device_id_type=MESH
            )

        copy = copy_from(src)
        if odd_src is None:
            copy.start()
        else:
            pl.when(k == 0)(copy.start)
            pl.when(k == 1)(copy_from(odd_src).start)
        copies.append(copy)
        return copy

    def piece(dx, dy):
        return kv_ref.at[:, lax.rem(x + dx, 4), lax.rem(y + dy, 4), k]

    def half(part, dx, dy):
        return kv_ref.at[part, lax.rem(x + dx, 4), lax.rem(y + dy, 4), k]

    middle = w_ref.shape[0] // 2
    halves = (pl.ds(0, middle), pl.ds(middle, middle))
    swapped = [
        pltpu.make_async_remote_copy(
            w_ref.at[halves[n]],
            wall_ref.at[x, halves[n]],
            own_sem.at[2 + n],
            own_sem.at[4 + n],
            device_id=(ctx_of(x, 3 - y, k), t),
            device_id_type=MESH,
        )
        for n in (0, 1)
    ]
    for copy in swapped:
        pl.when(k == 1)(copy.start)
    home = piece(0, 0)
    along = {d: remote(page_ref, home, at_x(d)) for d in (1, 3, 2)}
    up = {0: remote(page_ref, home, at_y(1))}
    down = {0: remote(page_ref, home, at_y(3))}
    shared = [remote(page_ref, home, other)]
    for d in (1, 3, 2):
        along[d].wait_recv()
        here = piece(4 - d, 0)
        up[d] = remote(here, here, at_y(1))
        down[d] = remote(here, here, at_y(3))
        shared.append(remote(here, here, other))
    for copy in swapped:
        pl.when(k == 1)(copy.wait_recv)
    right = {}
    left = {}
    for n in (0, 1):
        here = wall_ref.at[x, halves[n]]
        right[n] = remote(w_ref.at[halves[n]], here, at_x(1), here)
        here = wall_ref.at[x, halves[1 - n]]
        left[1 - n] = remote(w_ref.at[halves[1 - n]], here, at_x(3), here)
    far = {}
    far_w = []
    for d in (0, 1, 3, 2):
        dx = (4 - d) % 4
        up[d].wait_recv()
        here = half(0, dx, 3)
        far[0, d] = remote(here, here, at_y(1))
        shared.append(remote(piece(dx, 3), piece(dx, 3), other))
        down[d].wait_recv()
        here = half(1, dx, 1)
        far[1, d] = remote(here, here, at_y(3))
        shared.append(remote(piece(dx, 1), piece(dx, 1), other))
        if d == 3:
            right[0].wait_recv()
            here = wall_ref.at[lax.rem(x + 3, 4), halves[0]]
            far_w.append(remote(here, here, at_x(1)))
            left[1].wait_recv()
            here = wall_ref.at[lax.rem(x + 1, 4), halves[1]]
            far_w.append(remote(here, here, at_x(3)))
            far_w += [right[1], left[0]]
    for d in (0, 1, 3, 2):
        far[0, d].wait_recv()
        far[1, d].wait_recv()
        here = piece((4 - d) % 4, 2)
        shared.append(remote(here, here, other))
    for copy in far_w:
        copy.wait_recv()
    for copy in shared:
        copy.wait_recv()
    for copy in copies:
        copy.wait_send()
    for copy in swapped:
        pl.when(k == 1)(copy.wait_send)
    pl.when(k == 0)(kept.wait)
    own.wait()


GATHER_COPIES = 6 + 9 + 4 + 16 + 2 + 4


def gather_pages(page_cache, weights):
    rows = page_cache.shape[1]
    anywhere = pl.BlockSpec(memory_space=pl.ANY)
    return pl.pallas_call(
        gather_kernel,
        out_shape=(
            jax.ShapeDtypeStruct((2, 4, 4, 2, rows, HD), jnp.bfloat16),
            jax.ShapeDtypeStruct((4,) + weights.shape, jnp.bfloat16),
        ),
        in_specs=[anywhere, anywhere],
        out_specs=(anywhere, anywhere),
        scratch_shapes=[
            pltpu.SemaphoreType.DMA((6,)),
            pltpu.SemaphoreType.DMA((GATHER_COPIES,)),
            pltpu.SemaphoreType.DMA((GATHER_COPIES,)),
        ],
        compiler_params=pltpu.CompilerParams(collective_id=0, has_side_effects=True),
        name="gather_pages",
    )(page_cache, weights)


LANES = ((0, GROUP * PAGE),)
EXTRA = 16


def attention_kernel(
    slot_ref, parent_ref, count_ref, lost_ref, q_ref, new_ref, kv_ref, out_ref, keys, values, query, top, total,
    score_a, score_b, peak_a, peak_b
):
    scale = math.log2(math.e) / math.sqrt(HD)
    j = pl.program_id(0)
    base = lax.axis_index("ctx") * pl.num_programs(0)
    token = lax.broadcasted_iota(jnp.int32, (16, HD), 0)
    nt = (((1,), (1,)), ((), ()))

    def transposed(block):
        return block.T[: HD + EXTRA]

    def append(state):
        page, filled = state
        count = count_ref[page]
        first = slot_ref[page] * PAGE
        at = pl.ds(pl.multiple_of(first, PAGE), PAGE)
        to = pl.ds(pl.multiple_of(filled, 16), PAGE)
        keys[to, :] = kv_ref[0, at, :]
        values[to, :HD] = kv_ref[1, at, :]
        values[to, HD:] = jnp.ones((PAGE, HD), jnp.bfloat16)
        last = ((count - 1) // 16) * 16
        kept = token + last < count
        at = pl.ds(pl.multiple_of(first + last, 16), 16)
        to = pl.ds(pl.multiple_of(filled + last, 16), 16)
        lead = kv_ref[0, pl.ds(pl.multiple_of(first, PAGE), 16), :].astype(jnp.float32)[:1, :]
        keys[to, :] = jnp.where(kept, kv_ref[0, at, :].astype(jnp.float32), lead).astype(jnp.bfloat16)
        values[to, :HD] = jnp.where(kept, kv_ref[1, at, :].astype(jnp.float32), 0.0).astype(jnp.bfloat16)
        values[to, HD:] = kept.astype(jnp.float32).astype(jnp.bfloat16)
        return parent_ref[page], filled + last + 16

    unused_page, filled = lax.while_loop(
        lambda state: state[0] >= 0, append, (lost_ref[base + j], jnp.int32(0))
    )
    tail = pl.ds(pl.multiple_of(filled, 16), CHUNK)
    lead = keys[:16, :].astype(jnp.float32)[:1, :]
    keys[tail, :] = jnp.broadcast_to(lead, (CHUNK, HD)).astype(jnp.bfloat16)
    values[tail, :] = jnp.zeros((CHUNK, 2 * HD), jnp.bfloat16)
    for h in range(GROUP):
        query[h * PAGE : (h + 1) * PAGE, :] = q_ref[:, h * HD : (h + 1) * HD]

    with_ones = transposed(
        jnp.concatenate([new_ref[1], jnp.ones((PAGE, HD), jnp.bfloat16)], axis=1)
    )
    for start, width in LANES:
        lanes = pl.ds(start, width)
        score = lax.dot_general(
            new_ref[0], query[lanes, :], nt, preferred_element_type=jnp.float32
        )
        k_at = lax.broadcasted_iota(jnp.int32, (PAGE, width), 0)
        q_at = lax.broadcasted_iota(jnp.int32, (PAGE, width), 1) % PAGE
        seen = k_at <= q_at
        score = jnp.where(seen, score, -1e30)
        highest = jnp.max(score, axis=0, keepdims=True)
        weight = jnp.where(seen, jnp.exp2(score * scale - highest * scale), 0.0).astype(jnp.bfloat16)
        top[:, lanes] = jnp.broadcast_to(highest, (8, width))
        total[:, lanes] = jnp.dot(with_ones, weight, preferred_element_type=jnp.float32)

    def look(n, score_ref, peak_ref):
        at = pl.ds(pl.multiple_of(n * CHUNK, CHUNK), CHUNK)
        score = lax.dot_general(keys[at, :], query[...], nt, preferred_element_type=jnp.float32)
        score_ref[...] = score
        peak_ref[...] = jnp.broadcast_to(jnp.max(score, axis=0, keepdims=True), peak_ref.shape)

    def take(n, score_ref, peak_ref):
        at = pl.ds(pl.multiple_of(n * CHUNK, CHUNK), CHUNK)
        before = top[:1, :]
        highest = jnp.maximum(before, peak_ref[:1, :])
        weight = jnp.exp2(score_ref[...] * scale - highest * scale).astype(jnp.bfloat16)
        factor = jnp.exp2((before - highest) * scale)
        top[...] = jnp.broadcast_to(highest, top.shape)
        total[...] = total[...] * factor + jnp.dot(
            transposed(values[at, :]), weight, preferred_element_type=jnp.float32
        )

    def two_chunks(n, unused):
        look(2 * n + 1, score_b, peak_b)
        take(2 * n, score_a, peak_a)
        look(2 * n + 2, score_a, peak_a)
        take(2 * n + 1, score_b, peak_b)
        return unused

    chunks = (filled + CHUNK - 1) // CHUNK
    look(0, score_a, peak_a)
    lax.fori_loop(0, chunks // 2, two_chunks, 0)
    pl.when(chunks % 2 == 1)(lambda: take(chunks - 1, score_a, peak_a))
    for h in range(GROUP):
        lanes = pl.ds(h * PAGE, PAGE)
        out_ref[h * HD : (h + 1) * HD, :] = (total[:HD, lanes] / total[HD : HD + 1, lanes]).astype(
            jnp.bfloat16
        )


def attend(queries, new_kv, kv, page_slot, parent, valid_count, lost_parent):
    rows = kv.shape[1]
    smem = pl.BlockSpec(memory_space=pltpu.SMEM)
    vmem = pl.BlockSpec(memory_space=pltpu.VMEM)
    return pl.pallas_call(
        attention_kernel,
        out_shape=jax.ShapeDtypeStruct(queries.shape[::-1], jnp.bfloat16),
        grid=(queries.shape[0] // PAGE,),
        in_specs=[smem] * 4
        + [
            pl.BlockSpec((PAGE, queries.shape[1]), lambda j: (j, 0)),
            pl.BlockSpec((2, PAGE, HD), lambda j: (0, j, 0)),
            vmem,
        ],
        out_specs=pl.BlockSpec((queries.shape[1], PAGE), lambda j: (0, j)),
        scratch_shapes=[
            pltpu.VMEM((rows + 2 * CHUNK, HD), jnp.bfloat16),
            pltpu.VMEM((rows + CHUNK, 2 * HD), jnp.bfloat16),
            pltpu.VMEM((GROUP * PAGE, HD), jnp.bfloat16),
            pltpu.VMEM((8, GROUP * PAGE), jnp.float32),
            pltpu.VMEM((HD + EXTRA, GROUP * PAGE), jnp.float32),
            pltpu.VMEM((CHUNK, GROUP * PAGE), jnp.float32),
            pltpu.VMEM((CHUNK, GROUP * PAGE), jnp.float32),
            pltpu.VMEM((8, GROUP * PAGE), jnp.float32),
            pltpu.VMEM((8, GROUP * PAGE), jnp.float32),
        ],
        compiler_params=pltpu.CompilerParams(vmem_limit_bytes=VMEM_LIMIT),
        name="attend",
    )(page_slot, parent, valid_count, lost_parent, queries, new_kv, kv)


GROUPS = [
    (((0, 0, 0), (0, 0, 1)), 0.0),
    (((0, 1, 0), (0, 1, 1)), 0.4),
    (((1, 0, 0), (3, 0, 0)), 1.3),
    (((1, 1, 0), (3, 1, 0)), 1.8),
    (((1, 0, 1), (3, 0, 1)), 2.3),
    (((1, 1, 1), (3, 1, 1)), 2.7),
    (((2, 0, 0), (2, 1, 0)), 2.9),
    (((2, 0, 1), (2, 1, 1)), 3.5),
]
STEPS = 5
EVENTS = [(start - 0.05, parts, None) for parts, start in GROUPS]
EVENTS += [(start + step, parts, step) for parts, start in GROUPS for step in range(STEPS)]
EVENTS.sort(key=lambda event: event[0])
EVEN = ((4, None, 0), (-2, 2, 2), (2, 0, 1))
ODD = ((-3, None, 2), (3, 0, 0), (-1, 2, 3), (1, 1, 1))


def project_kernel(
    own_ref, all_ref, out_ref, att_ref, w_ref, peers, terms, outgoing, incoming, load_sem,
    a_send, a_recv, z_send, z_recv, f_send, f_recv
):
    x, y, k, t = place()
    here = ctx_of(x, y, k)

    def holder(dy, dk):
        return (ctx_of(x, lax.rem(y + dy, 4), k if dk == 0 else 1 - k), t)

    loads = [
        pltpu.make_async_copy(own_ref, att_ref, load_sem.at[0]),
        pltpu.make_async_copy(all_ref, w_ref, load_sem.at[1]),
    ]
    for copy in loads:
        copy.start()
    columns = w_ref.shape[0] // 4
    width = att_ref.shape[1] // 2
    lanes = (pl.ds(0, width), pl.ds(width, width))
    mine = lax.rem(y + k, 2) * 2 + k
    odd = lax.rem(t + lax.div(y, 2) + k, 2)
    barrier = pltpu.get_barrier_semaphore()
    others = [(dy, dk) for dy in range(4) for dk in range(2) if (dy, dk) != (0, 0)]
    for device in [holder(dy, dk) for dy, dk in others] + [(here, lax.rem(t + 1, 8)), (here, lax.rem(t + 7, 8))]:
        pl.semaphore_signal(barrier, inc=1, device_id=device, device_id_type=MESH)
    pl.semaphore_wait(barrier, 9)

    def share(src, dy, dk, side, device):
        copy = pltpu.make_async_remote_copy(
            src,
            peers.at[dy, dk, side],
            a_send.at[dy, dk, side],
            a_recv.at[dy, dk, side],
            device_id=device,
            device_id_type=MESH,
        )
        copy.start()
        return copy

    shared = {}

    def share_near(side):
        mine_here = own_ref.at[:, lanes[side]]
        shared[3, 0, side] = share(mine_here, 3, 0, side, holder(1, 0))
        shared[1, 0, side] = share(mine_here, 1, 0, side, holder(3, 0))

    share_near(0)
    for side in (0, 1):
        shared[0, 1, side] = share(own_ref.at[:, lanes[side]], 0, 1, side, holder(0, 1))

    def need(dy, dk, side):
        if (dy, dk) == (0, 0):
            return
        shared[dy, dk, side].wait_recv()
        if dk == 0:
            if dy == (3 if side == 0 else 1):
                shared[2, 0, side] = share(peers.at[dy, 0, side], 2, 0, side, holder(4 - dy, 0))
            shared[dy, 1, side] = share(peers.at[dy, 0, side], dy, 1, side, holder(0, 1))

    def long_way(dk):
        return (1 - 2 * k) * (1 - 2 * dk)

    def hop(part, i, arm, slot):
        dy, dk, side = part
        step = long_way(dk) if arm > 0 else -long_way(dk)
        return pltpu.make_async_remote_copy(
            outgoing.at[dy, dk, i, side],
            incoming.at[dy, dk, slot, side],
            z_send.at[dy, dk, i, side],
            z_recv.at[dy, dk, slot, side],
            device_id=(here, lax.rem(t + step + 8, 8)),
            device_id_type=MESH,
        )

    def arrived(part, slot):
        dy, dk, side = part
        spot = incoming.at[dy, dk, slot, side]
        pltpu.make_async_copy(spot, spot, z_recv.at[dy, dk, slot, side]).wait()
        return incoming[dy, dk, slot, side].astype(jnp.float32)

    spot = pl.ds(pl.multiple_of(mine * columns, 16), columns)

    def result(part):
        dy, dk, side = part
        return pltpu.make_async_remote_copy(
            outgoing.at[dy, dk, 3, side],
            out_ref.at[spot, lanes[side]],
            f_send.at[dy, dk, side],
            f_recv.at[mine, side],
            device_id=holder(dy, dk),
            device_id_type=MESH,
        )

    def term(part, distance):
        dy, dk, side = part
        target = lax.rem(t + long_way(dk) * distance + 8, 8)
        at = pl.ds(pl.multiple_of(lax.div(target, 2) * columns, 32), columns)
        return terms[dy, dk, side, at, :]

    def pass_on(parts, i, table):
        distance, source, slot = table[i]
        for part in parts:
            dy, dk, side = part
            total = term(part, distance)
            if source is not None:
                total = total + arrived(part, source)
            outgoing[dy, dk, i, side] = total.astype(jnp.bfloat16)
            hop(part, i, distance, slot).start()

    def finish(parts):
        for part in parts:
            dy, dk, side = part
            total = term(part, 0) + arrived(part, 3) + arrived(part, 1)
            if (dy, dk) == (0, 0):
                out_ref[spot, lanes[side]] = total.astype(jnp.bfloat16)
            else:
                outgoing[dy, dk, 3, side] = total.astype(jnp.bfloat16)
                result(part).start()

    def multiply(parts):
        for part in parts:
            need(*part)
        if parts[0][:2] == (0, 0):
            rows = att_ref[...]
        else:
            rows = jnp.concatenate([peers[part] for part in parts], axis=1)
        products = jnp.dot(w_ref[...], rows, preferred_element_type=jnp.float32)
        for n, (dy, dk, side) in enumerate(parts):
            terms[dy, dk, side] = products[:, n * width : (n + 1) * width]

    for copy in loads:
        copy.wait()
    for unused_time, parts, i in EVENTS:
        if i is None:
            if parts[0][0] == 1 and (1, 0, 1) not in shared:
                share_near(1)
            multiply(parts)
            continue
        if i < 4:
            pl.when(odd == 1)(lambda parts=parts, i=i: pass_on(parts, i, ODD))
        if i < 3:
            pl.when(odd == 0)(lambda parts=parts, i=i: pass_on(parts, i, EVEN))
        if i == 4:
            pl.when(odd == 0)(lambda parts=parts: finish(parts))

    for n in range(4):

        @pl.when((odd == 1) | (mine != n))
        def _(n=n):
            for side in (0, 1):
                landed = out_ref.at[pl.ds(n * columns, columns), lanes[side]]
                pltpu.make_async_copy(landed, landed, f_recv.at[n, side]).wait()

    for copy in shared.values():
        copy.wait_send()

    def drain(part, table):
        for i, (distance, source, slot) in enumerate(table):
            hop(part, i, distance, slot).wait_send()

    for parts, unused_start in GROUPS:
        for part in parts:
            pl.when(odd == 1)(lambda part=part: drain(part, ODD))

            @pl.when(odd == 0)
            def _(part=part):
                drain(part, EVEN)
                if part[:2] != (0, 0):
                    result(part).wait_send()


def project(attended, weights):
    depth, rows = attended.shape
    columns = weights.shape[0] // 4
    vmem = pl.BlockSpec(memory_space=pltpu.VMEM)
    return pl.pallas_call(
        project_kernel,
        out_shape=jax.ShapeDtypeStruct((4 * columns, rows), jnp.bfloat16),
        in_specs=[pl.BlockSpec(memory_space=pl.ANY)] * 2,
        out_specs=vmem,
        scratch_shapes=[
            pltpu.VMEM((depth, rows), jnp.bfloat16),
            pltpu.VMEM(weights.shape, jnp.bfloat16),
            pltpu.VMEM((4, 2, 2, depth, rows // 2), jnp.bfloat16),
            pltpu.VMEM((4, 2, 2, 4 * columns, rows // 2), jnp.float32),
            pltpu.VMEM((4, 2, 4, 2, columns, rows // 2), jnp.bfloat16),
            pltpu.VMEM((4, 2, 4, 2, columns, rows // 2), jnp.bfloat16),
            pltpu.SemaphoreType.DMA((2,)),
            pltpu.SemaphoreType.DMA((4, 2, 2)),
            pltpu.SemaphoreType.DMA((4, 2, 2)),
            pltpu.SemaphoreType.DMA((4, 2, 4, 2)),
            pltpu.SemaphoreType.DMA((4, 2, 4, 2)),
            pltpu.SemaphoreType.DMA((4, 2, 2)),
            pltpu.SemaphoreType.DMA((4, 2)),
        ],
        compiler_params=pltpu.CompilerParams(
            collective_id=1, has_side_effects=True, vmem_limit_bytes=VMEM_LIMIT
        ),
        name="project",
    )(attended, weights)


def per_device(
    queries, new_kv, page_cache, out_weight, page_slot, parent, valid_count, lost_parent
):
    kv, weights = gather_pages(page_cache, out_weight.T)
    kv = kv.reshape(2, -1, HD)
    attended = attend(queries, new_kv, kv, page_slot, parent, valid_count, lost_parent)
    return project(attended, weights.reshape(-1, weights.shape[2])).T


def solution(mesh):
    return jax.shard_map(
        per_device,
        mesh=mesh,
        in_specs=(
            P("ctx", "tp"),
            P(None, "ctx", "tp"),
            P(None, "ctx", "tp"),
            P("tp", "ctx"),
            P(),
            P(),
            P(),
            P(),
        ),
        out_specs=P("ctx", "tp"),
        check_vma=False,
    )
```

```python
import math

import jax
import jax.numpy as jnp
from jax import lax
from jax.experimental import pallas as pl
from jax.experimental.pallas import tpu as pltpu
from jax.sharding import PartitionSpec as P

HEADS = 56
KV_HEADS = 8
HD = 128
PAGE = 128
GROUP = HEADS // KV_HEADS
CHUNK = 512
MESH = pl.DeviceIdType.MESH
VMEM_LIMIT = 56 * 2**20


def place():
    c = lax.axis_index("ctx")
    return lax.div(c, 8), lax.rem(lax.div(c, 2), 4), lax.rem(c, 2), lax.axis_index("tp")


def ctx_of(x, y, k):
    return (x * 4 + y) * 2 + k


def gather_kernel(page_ref, w_ref, kv_ref, wall_ref, own_sem, send_sem, recv_sem):
    x, y, k, t = place()

    def at_x(d):
        return (ctx_of(lax.rem(x + d, 4), y, k), t)

    def at_y(d):
        return (ctx_of(x, lax.rem(y + d, 4), k), t)

    other = (ctx_of(x, y, 1 - k), t)
    barrier = pltpu.get_barrier_semaphore()
    for device in (at_x(1), at_x(2), at_x(3), at_y(1), at_y(2), at_y(3), other):
        pl.semaphore_signal(barrier, inc=1, device_id=device, device_id_type=MESH)
    own = pltpu.make_async_copy(page_ref, kv_ref.at[:, x, y, k], own_sem.at[0])
    own.start()
    kept = pltpu.make_async_copy(w_ref, wall_ref.at[x], own_sem.at[1])
    pl.when(k == 0)(kept.start)
    pl.semaphore_wait(barrier, 7)

    copies = []

    def remote(src, dst, device, odd_src=None):
        n = len(copies)

        def copy_from(ref):
            return pltpu.make_async_remote_copy(
                ref, dst, send_sem.at[n], recv_sem.at[n], device_id=device, device_id_type=MESH
            )

        copy = copy_from(src)
        if odd_src is None:
            copy.start()
        else:
            pl.when(k == 0)(copy.start)
            pl.when(k == 1)(copy_from(odd_src).start)
        copies.append(copy)
        return copy

    def piece(dx, dy):
        return kv_ref.at[:, lax.rem(x + dx, 4), lax.rem(y + dy, 4), k]

    def half(part, dx, dy):
        return kv_ref.at[part, lax.rem(x + dx, 4), lax.rem(y + dy, 4), k]

    middle = w_ref.shape[0] // 2
    halves = (pl.ds(0, middle), pl.ds(middle, middle))
    swapped = [
        pltpu.make_async_remote_copy(
            w_ref.at[halves[n]],
            wall_ref.at[x, halves[n]],
            own_sem.at[2 + n],
            own_sem.at[4 + n],
            device_id=(ctx_of(x, 3 - y, k), t),
            device_id_type=MESH,
        )
        for n in (0, 1)
    ]
    for copy in swapped:
        pl.when(k == 1)(copy.start)
    home = piece(0, 0)
    along = {d: remote(page_ref, home, at_x(d)) for d in (1, 3, 2)}
    up = {0: remote(page_ref, home, at_y(1))}
    down = {0: remote(page_ref, home, at_y(3))}
    shared = [remote(page_ref, home, other)]
    for d in (1, 3, 2):
        along[d].wait_recv()
        here = piece(4 - d, 0)
        up[d] = remote(here, here, at_y(1))
        down[d] = remote(here, here, at_y(3))
        shared.append(remote(here, here, other))
    for copy in swapped:
        pl.when(k == 1)(copy.wait_recv)
    right = {}
    left = {}
    for n in (0, 1):
        here = wall_ref.at[x, halves[n]]
        right[n] = remote(w_ref.at[halves[n]], here, at_x(1), here)
        here = wall_ref.at[x, halves[1 - n]]
        left[1 - n] = remote(w_ref.at[halves[1 - n]], here, at_x(3), here)
    far = {}
    far_w = []
    for d in (0, 1, 3, 2):
        dx = (4 - d) % 4
        up[d].wait_recv()
        here = half(0, dx, 3)
        far[0, d] = remote(here, here, at_y(1))
        shared.append(remote(piece(dx, 3), piece(dx, 3), other))
        down[d].wait_recv()
        here = half(1, dx, 1)
        far[1, d] = remote(here, here, at_y(3))
        shared.append(remote(piece(dx, 1), piece(dx, 1), other))
        if d == 3:
            right[0].wait_recv()
            here = wall_ref.at[lax.rem(x + 3, 4), halves[0]]
            far_w.append(remote(here, here, at_x(1)))
            left[1].wait_recv()
            here = wall_ref.at[lax.rem(x + 1, 4), halves[1]]
            far_w.append(remote(here, here, at_x(3)))
            far_w += [right[1], left[0]]
    for d in (0, 1, 3, 2):
        far[0, d].wait_recv()
        far[1, d].wait_recv()
        here = piece((4 - d) % 4, 2)
        shared.append(remote(here, here, other))
    for copy in far_w:
        copy.wait_recv()
    for copy in shared:
        copy.wait_recv()
    for copy in copies:
        copy.wait_send()
    for copy in swapped:
        pl.when(k == 1)(copy.wait_send)
    pl.when(k == 0)(kept.wait)
    own.wait()


GATHER_COPIES = 6 + 9 + 4 + 16 + 2 + 4


def gather_pages(page_cache, weights):
    rows = page_cache.shape[1]
    anywhere = pl.BlockSpec(memory_space=pl.ANY)
    return pl.pallas_call(
        gather_kernel,
        out_shape=(
            jax.ShapeDtypeStruct((2, 4, 4, 2, rows, HD), jnp.bfloat16),
            jax.ShapeDtypeStruct((4,) + weights.shape, jnp.bfloat16),
        ),
        in_specs=[anywhere, anywhere],
        out_specs=(anywhere, anywhere),
        scratch_shapes=[
            pltpu.SemaphoreType.DMA((6,)),
            pltpu.SemaphoreType.DMA((GATHER_COPIES,)),
            pltpu.SemaphoreType.DMA((GATHER_COPIES,)),
        ],
        compiler_params=pltpu.CompilerParams(collective_id=0, has_side_effects=True),
        name="gather_pages",
    )(page_cache, weights)


LANES = ((0, GROUP * PAGE),)
EXTRA = 16


def attention_kernel(
    slot_ref, parent_ref, count_ref, lost_ref, q_ref, new_ref, kv_ref, out_ref, keys, values, query, top, total,
    score_a, score_b, peak_a, peak_b
):
    scale = math.log2(math.e) / math.sqrt(HD)
    j = pl.program_id(0)
    base = lax.axis_index("ctx") * pl.num_programs(0)
    token = lax.broadcasted_iota(jnp.int32, (16, HD), 0)
    nt = (((1,), (1,)), ((), ()))

    def transposed(block):
        return block.T[: HD + EXTRA]

    def append(state):
        page, filled = state
        count = count_ref[page]
        first = slot_ref[page] * PAGE
        at = pl.ds(pl.multiple_of(first, PAGE), PAGE)
        to = pl.ds(pl.multiple_of(filled, 16), PAGE)
        keys[to, :] = kv_ref[0, at, :]
        values[to, :HD] = kv_ref[1, at, :]
        values[to, HD:] = jnp.ones((PAGE, HD), jnp.bfloat16)
        last = ((count - 1) // 16) * 16
        kept = token + last < count
        at = pl.ds(pl.multiple_of(first + last, 16), 16)
        to = pl.ds(pl.multiple_of(filled + last, 16), 16)
        lead = kv_ref[0, pl.ds(pl.multiple_of(first, PAGE), 16), :].astype(jnp.float32)[:1, :]
        keys[to, :] = jnp.where(kept, kv_ref[0, at, :].astype(jnp.float32), lead).astype(jnp.bfloat16)
        values[to, :HD] = jnp.where(kept, kv_ref[1, at, :].astype(jnp.float32), 0.0).astype(jnp.bfloat16)
        values[to, HD:] = kept.astype(jnp.float32).astype(jnp.bfloat16)
        return parent_ref[page], filled + last + 16

    unused_page, filled = lax.while_loop(
        lambda state: state[0] >= 0, append, (lost_ref[base + j], jnp.int32(0))
    )
    tail = pl.ds(pl.multiple_of(filled, 16), CHUNK)
    lead = keys[:16, :].astype(jnp.float32)[:1, :]
    keys[tail, :] = jnp.broadcast_to(lead, (CHUNK, HD)).astype(jnp.bfloat16)
    values[tail, :] = jnp.zeros((CHUNK, 2 * HD), jnp.bfloat16)
    for h in range(GROUP):
        query[h * PAGE : (h + 1) * PAGE, :] = q_ref[:, h * HD : (h + 1) * HD]

    with_ones = transposed(
        jnp.concatenate([new_ref[1], jnp.ones((PAGE, HD), jnp.bfloat16)], axis=1)
    )
    for start, width in LANES:
        lanes = pl.ds(start, width)
        score = lax.dot_general(
            new_ref[0], query[lanes, :], nt, preferred_element_type=jnp.float32
        )
        k_at = lax.broadcasted_iota(jnp.int32, (PAGE, width), 0)
        q_at = lax.broadcasted_iota(jnp.int32, (PAGE, width), 1) % PAGE
        seen = k_at <= q_at
        score = jnp.where(seen, score, -1e30)
        highest = jnp.max(score, axis=0, keepdims=True)
        weight = jnp.where(seen, jnp.exp2(score * scale - highest * scale), 0.0).astype(jnp.bfloat16)
        top[:, lanes] = jnp.broadcast_to(highest, (8, width))
        total[:, lanes] = jnp.dot(with_ones, weight, preferred_element_type=jnp.float32)

    def look(n, score_ref, peak_ref):
        at = pl.ds(pl.multiple_of(n * CHUNK, CHUNK), CHUNK)
        score = lax.dot_general(keys[at, :], query[...], nt, preferred_element_type=jnp.float32)
        score_ref[...] = score
        peak_ref[...] = jnp.broadcast_to(jnp.max(score, axis=0, keepdims=True), peak_ref.shape)

    def take(n, score_ref, peak_ref):
        at = pl.ds(pl.multiple_of(n * CHUNK, CHUNK), CHUNK)
        before = top[:1, :]
        highest = jnp.maximum(before, peak_ref[:1, :])
        weight = jnp.exp2(score_ref[...] * scale - highest * scale).astype(jnp.bfloat16)
        factor = jnp.exp2((before - highest) * scale)
        top[...] = jnp.broadcast_to(highest, top.shape)
        total[...] = total[...] * factor + jnp.dot(
            transposed(values[at, :]), weight, preferred_element_type=jnp.float32
        )

    def two_chunks(n, unused):
        look(2 * n + 1, score_b, peak_b)
        take(2 * n, score_a, peak_a)
        look(2 * n + 2, score_a, peak_a)
        take(2 * n + 1, score_b, peak_b)
        return unused

    chunks = (filled + CHUNK - 1) // CHUNK
    look(0, score_a, peak_a)
    lax.fori_loop(0, chunks // 2, two_chunks, 0)
    pl.when(chunks % 2 == 1)(lambda: take(chunks - 1, score_a, peak_a))
    for h in range(GROUP):
        lanes = pl.ds(h * PAGE, PAGE)
        out_ref[h * HD : (h + 1) * HD, :] = (total[:HD, lanes] / total[HD : HD + 1, lanes]).astype(
            jnp.bfloat16
        )


def attend(queries, new_kv, kv, page_slot, parent, valid_count, lost_parent):
    rows = kv.shape[1]
    smem = pl.BlockSpec(memory_space=pltpu.SMEM)
    vmem = pl.BlockSpec(memory_space=pltpu.VMEM)
    return pl.pallas_call(
        attention_kernel,
        out_shape=jax.ShapeDtypeStruct(queries.shape[::-1], jnp.bfloat16),
        grid=(queries.shape[0] // PAGE,),
        in_specs=[smem] * 4
        + [
            pl.BlockSpec((PAGE, queries.shape[1]), lambda j: (j, 0)),
            pl.BlockSpec((2, PAGE, HD), lambda j: (0, j, 0)),
            vmem,
        ],
        out_specs=pl.BlockSpec((queries.shape[1], PAGE), lambda j: (0, j)),
        scratch_shapes=[
            pltpu.VMEM((rows + 2 * CHUNK, HD), jnp.bfloat16),
            pltpu.VMEM((rows + CHUNK, 2 * HD), jnp.bfloat16),
            pltpu.VMEM((GROUP * PAGE, HD), jnp.bfloat16),
            pltpu.VMEM((8, GROUP * PAGE), jnp.float32),
            pltpu.VMEM((HD + EXTRA, GROUP * PAGE), jnp.float32),
            pltpu.VMEM((CHUNK, GROUP * PAGE), jnp.float32),
            pltpu.VMEM((CHUNK, GROUP * PAGE), jnp.float32),
            pltpu.VMEM((8, GROUP * PAGE), jnp.float32),
            pltpu.VMEM((8, GROUP * PAGE), jnp.float32),
        ],
        compiler_params=pltpu.CompilerParams(vmem_limit_bytes=VMEM_LIMIT),
        name="attend",
    )(page_slot, parent, valid_count, lost_parent, queries, new_kv, kv)


GROUPS = [
    (((0, 0, 0), (0, 0, 1)), 0.0),
    (((0, 1, 0), (0, 1, 1)), 0.4),
    (((1, 0, 0), (3, 0, 0)), 1.3),
    (((1, 1, 0), (3, 1, 0)), 1.8),
    (((1, 0, 1), (3, 0, 1)), 2.3),
    (((1, 1, 1), (3, 1, 1)), 2.7),
    (((2, 0, 0), (2, 1, 0)), 2.9),
    (((2, 0, 1), (2, 1, 1)), 3.5),
]
STEPS = 5
EVENTS = [(start - 0.05, parts, None) for parts, start in GROUPS]
EVENTS += [(start + step, parts, step) for parts, start in GROUPS for step in range(STEPS)]
EVENTS.sort(key=lambda event: event[0])
EVEN = ((4, None, 0), (-2, 2, 2), (2, 0, 1))
ODD = ((-3, None, 2), (3, 0, 0), (-1, 2, 3), (1, 1, 1))


def project_kernel(
    own_ref, all_ref, out_ref, att_ref, w_ref, peers, terms, outgoing, incoming, load_sem,
    a_send, a_recv, z_send, z_recv, f_send, f_recv
):
    x, y, k, t = place()
    here = ctx_of(x, y, k)

    def holder(dy, dk):
        return (ctx_of(x, lax.rem(y + dy, 4), k if dk == 0 else 1 - k), t)

    loads = [
        pltpu.make_async_copy(own_ref, att_ref, load_sem.at[0]),
        pltpu.make_async_copy(all_ref, w_ref, load_sem.at[1]),
    ]
    for copy in loads:
        copy.start()
    columns = w_ref.shape[0] // 4
    width = att_ref.shape[1] // 2
    lanes = (pl.ds(0, width), pl.ds(width, width))
    mine = lax.rem(y + k, 2) * 2 + k
    odd = lax.rem(t + lax.div(y, 2) + k, 2)
    barrier = pltpu.get_barrier_semaphore()
    others = [(dy, dk) for dy in range(4) for dk in range(2) if (dy, dk) != (0, 0)]
    for device in [holder(dy, dk) for dy, dk in others] + [(here, lax.rem(t + 1, 8)), (here, lax.rem(t + 7, 8))]:
        pl.semaphore_signal(barrier, inc=1, device_id=device, device_id_type=MESH)
    pl.semaphore_wait(barrier, 9)

    def share(src, dy, dk, side, device):
        copy = pltpu.make_async_remote_copy(
            src,
            peers.at[dy, dk, side],
            a_send.at[dy, dk, side],
            a_recv.at[dy, dk, side],
            device_id=device,
            device_id_type=MESH,
        )
        copy.start()
        return copy

    shared = {}

    def share_near(side):
        mine_here = own_ref.at[:, lanes[side]]
        shared[3, 0, side] = share(mine_here, 3, 0, side, holder(1, 0))
        shared[1, 0, side] = share(mine_here, 1, 0, side, holder(3, 0))

    share_near(0)
    for side in (0, 1):
        shared[0, 1, side] = share(own_ref.at[:, lanes[side]], 0, 1, side, holder(0, 1))

    def need(dy, dk, side):
        if (dy, dk) == (0, 0):
            return
        shared[dy, dk, side].wait_recv()
        if dk == 0:
            if dy == (3 if side == 0 else 1):
                shared[2, 0, side] = share(peers.at[dy, 0, side], 2, 0, side, holder(4 - dy, 0))
            shared[dy, 1, side] = share(peers.at[dy, 0, side], dy, 1, side, holder(0, 1))

    def long_way(part):
        dy, dk, side = part
        return (1 - 2 * k) * (-1 if (dk + side + (dy == 3)) % 2 else 1)

    def hop(part, i, arm, slot):
        dy, dk, side = part
        step = long_way(part) if arm > 0 else -long_way(part)
        return pltpu.make_async_remote_copy(
            outgoing.at[dy, dk, i, side],
            incoming.at[dy, dk, slot, side],
            z_send.at[dy, dk, i, side],
            z_recv.at[dy, dk, slot, side],
            device_id=(here, lax.rem(t + step + 8, 8)),
            device_id_type=MESH,
        )

    def arrived(part, slot):
        dy, dk, side = part
        spot = incoming.at[dy, dk, slot, side]
        pltpu.make_async_copy(spot, spot, z_recv.at[dy, dk, slot, side]).wait()
        return incoming[dy, dk, slot, side].astype(jnp.float32)

    spot = pl.ds(pl.multiple_of(mine * columns, 16), columns)

    def result(part):
        dy, dk, side = part
        return pltpu.make_async_remote_copy(
            outgoing.at[dy, dk, 3, side],
            out_ref.at[spot, lanes[side]],
            f_send.at[dy, dk, side],
            f_recv.at[mine, side],
            device_id=holder(dy, dk),
            device_id_type=MESH,
        )

    def term(part, distance):
        dy, dk, side = part
        target = lax.rem(t + long_way(part) * distance + 8, 8)
        at = pl.ds(pl.multiple_of(lax.div(target, 2) * columns, 32), columns)
        return terms[dy, dk, side, at, :]

    def pass_on(parts, i, table):
        distance, source, slot = table[i]
        for part in parts:
            dy, dk, side = part
            total = term(part, distance)
            if source is not None:
                total = total + arrived(part, source)
            outgoing[dy, dk, i, side] = total.astype(jnp.bfloat16)
            hop(part, i, distance, slot).start()

    def finish(parts):
        for part in parts:
            dy, dk, side = part
            total = term(part, 0) + arrived(part, 3) + arrived(part, 1)
            if (dy, dk) == (0, 0):
                out_ref[spot, lanes[side]] = total.astype(jnp.bfloat16)
            else:
                outgoing[dy, dk, 3, side] = total.astype(jnp.bfloat16)
                result(part).start()

    def multiply(parts):
        for part in parts:
            need(*part)
        if parts[0][:2] == (0, 0):
            rows = att_ref[...]
        else:
            rows = jnp.concatenate([peers[part] for part in parts], axis=1)
        products = jnp.dot(w_ref[...], rows, preferred_element_type=jnp.float32)
        for n, (dy, dk, side) in enumerate(parts):
            terms[dy, dk, side] = products[:, n * width : (n + 1) * width]

    for copy in loads:
        copy.wait()
    for unused_time, parts, i in EVENTS:
        if i is None:
            if parts[0][0] == 1 and (1, 0, 1) not in shared:
                share_near(1)
            multiply(parts)
            continue
        if i < 4:
            pl.when(odd == 1)(lambda parts=parts, i=i: pass_on(parts, i, ODD))
        if i < 3:
            pl.when(odd == 0)(lambda parts=parts, i=i: pass_on(parts, i, EVEN))
        if i == 4:
            pl.when(odd == 0)(lambda parts=parts: finish(parts))

    for n in range(4):

        @pl.when((odd == 1) | (mine != n))
        def _(n=n):
            for side in (0, 1):
                landed = out_ref.at[pl.ds(n * columns, columns), lanes[side]]
                pltpu.make_async_copy(landed, landed, f_recv.at[n, side]).wait()

    for copy in shared.values():
        copy.wait_send()

    def drain(part, table):
        for i, (distance, source, slot) in enumerate(table):
            hop(part, i, distance, slot).wait_send()

    for parts, unused_start in GROUPS:
        for part in parts:
            pl.when(odd == 1)(lambda part=part: drain(part, ODD))

            @pl.when(odd == 0)
            def _(part=part):
                drain(part, EVEN)
                if part[:2] != (0, 0):
                    result(part).wait_send()


def project(attended, weights):
    depth, rows = attended.shape
    columns = weights.shape[0] // 4
    vmem = pl.BlockSpec(memory_space=pltpu.VMEM)
    return pl.pallas_call(
        project_kernel,
        out_shape=jax.ShapeDtypeStruct((4 * columns, rows), jnp.bfloat16),
        in_specs=[pl.BlockSpec(memory_space=pl.ANY)] * 2,
        out_specs=vmem,
        scratch_shapes=[
            pltpu.VMEM((depth, rows), jnp.bfloat16),
            pltpu.VMEM(weights.shape, jnp.bfloat16),
            pltpu.VMEM((4, 2, 2, depth, rows // 2), jnp.bfloat16),
            pltpu.VMEM((4, 2, 2, 4 * columns, rows // 2), jnp.float32),
            pltpu.VMEM((4, 2, 4, 2, columns, rows // 2), jnp.bfloat16),
            pltpu.VMEM((4, 2, 4, 2, columns, rows // 2), jnp.bfloat16),
            pltpu.SemaphoreType.DMA((2,)),
            pltpu.SemaphoreType.DMA((4, 2, 2)),
            pltpu.SemaphoreType.DMA((4, 2, 2)),
            pltpu.SemaphoreType.DMA((4, 2, 4, 2)),
            pltpu.SemaphoreType.DMA((4, 2, 4, 2)),
            pltpu.SemaphoreType.DMA((4, 2, 2)),
            pltpu.SemaphoreType.DMA((4, 2)),
        ],
        compiler_params=pltpu.CompilerParams(
            collective_id=1, has_side_effects=True, vmem_limit_bytes=VMEM_LIMIT
        ),
        name="project",
    )(attended, weights)


def per_device(
    queries, new_kv, page_cache, out_weight, page_slot, parent, valid_count, lost_parent
):
    kv, weights = gather_pages(page_cache, out_weight.T)
    kv = kv.reshape(2, -1, HD)
    attended = attend(queries, new_kv, kv, page_slot, parent, valid_count, lost_parent)
    return project(attended, weights.reshape(-1, weights.shape[2])).T


def solution(mesh):
    return jax.shard_map(
        per_device,
        mesh=mesh,
        in_specs=(
            P("ctx", "tp"),
            P(None, "ctx", "tp"),
            P(None, "ctx", "tp"),
            P("tp", "ctx"),
            P(),
            P(),
            P(),
            P(),
        ),
        out_specs=P("ctx", "tp"),
        check_vma=False,
    )
```

```python
import math

import jax
import jax.numpy as jnp
from jax import lax
from jax.experimental import pallas as pl
from jax.experimental.pallas import tpu as pltpu
from jax.sharding import PartitionSpec as P

HEADS = 56
KV_HEADS = 8
HD = 128
PAGE = 128
GROUP = HEADS // KV_HEADS
CHUNK = 512
MESH = pl.DeviceIdType.MESH
VMEM_LIMIT = 56 * 2**20


def place():
    c = lax.axis_index("ctx")
    return lax.div(c, 8), lax.rem(lax.div(c, 2), 4), lax.rem(c, 2), lax.axis_index("tp")


def ctx_of(x, y, k):
    return (x * 4 + y) * 2 + k


def gather_kernel(page_ref, w_ref, kv_ref, wall_ref, own_sem, send_sem, recv_sem):
    x, y, k, t = place()

    def at_x(d):
        return (ctx_of(lax.rem(x + d, 4), y, k), t)

    def at_y(d):
        return (ctx_of(x, lax.rem(y + d, 4), k), t)

    other = (ctx_of(x, y, 1 - k), t)
    barrier = pltpu.get_barrier_semaphore()
    for device in (at_x(1), at_x(2), at_x(3), at_y(1), at_y(2), at_y(3), other):
        pl.semaphore_signal(barrier, inc=1, device_id=device, device_id_type=MESH)
    own = pltpu.make_async_copy(page_ref, kv_ref.at[:, x, y, k], own_sem.at[0])
    own.start()
    kept = pltpu.make_async_copy(w_ref, wall_ref.at[x], own_sem.at[1])
    pl.when(k == 0)(kept.start)
    pl.semaphore_wait(barrier, 7)

    copies = []

    def remote(src, dst, device, odd_src=None):
        n = len(copies)

        def copy_from(ref):
            return pltpu.make_async_remote_copy(
                ref, dst, send_sem.at[n], recv_sem.at[n], device_id=device, device_id_type=MESH
            )

        copy = copy_from(src)
        if odd_src is None:
            copy.start()
        else:
            pl.when(k == 0)(copy.start)
            pl.when(k == 1)(copy_from(odd_src).start)
        copies.append(copy)
        return copy

    def piece(dx, dy):
        return kv_ref.at[:, lax.rem(x + dx, 4), lax.rem(y + dy, 4), k]

    def half(part, dx, dy):
        return kv_ref.at[part, lax.rem(x + dx, 4), lax.rem(y + dy, 4), k]

    middle = w_ref.shape[0] // 2
    halves = (pl.ds(0, middle), pl.ds(middle, middle))
    swapped = [
        pltpu.make_async_remote_copy(
            w_ref.at[halves[n]],
            wall_ref.at[x, halves[n]],
            own_sem.at[2 + n],
            own_sem.at[4 + n],
            device_id=(ctx_of(x, 3 - y, k), t),
            device_id_type=MESH,
        )
        for n in (0, 1)
    ]
    for copy in swapped:
        pl.when(k == 1)(copy.start)
    home = piece(0, 0)
    along = {d: remote(page_ref, home, at_x(d)) for d in (1, 3, 2)}
    up = {0: remote(page_ref, home, at_y(1))}
    down = {0: remote(page_ref, home, at_y(3))}
    shared = [remote(page_ref, home, other)]
    for d in (1, 3, 2):
        along[d].wait_recv()
        here = piece(4 - d, 0)
        up[d] = remote(here, here, at_y(1))
        down[d] = remote(here, here, at_y(3))
        shared.append(remote(here, here, other))
    for copy in swapped:
        pl.when(k == 1)(copy.wait_recv)
    right = {}
    left = {}
    for n in (0, 1):
        here = wall_ref.at[x, halves[n]]
        right[n] = remote(w_ref.at[halves[n]], here, at_x(1), here)
        here = wall_ref.at[x, halves[1 - n]]
        left[1 - n] = remote(w_ref.at[halves[1 - n]], here, at_x(3), here)
    far = {}
    far_w = []
    for d in (0, 1, 3, 2):
        dx = (4 - d) % 4
        up[d].wait_recv()
        here = half(0, dx, 3)
        far[0, d] = remote(here, here, at_y(1))
        shared.append(remote(piece(dx, 3), piece(dx, 3), other))
        down[d].wait_recv()
        here = half(1, dx, 1)
        far[1, d] = remote(here, here, at_y(3))
        shared.append(remote(piece(dx, 1), piece(dx, 1), other))
        if d == 3:
            right[0].wait_recv()
            here = wall_ref.at[lax.rem(x + 3, 4), halves[0]]
            far_w.append(remote(here, here, at_x(1)))
            left[1].wait_recv()
            here = wall_ref.at[lax.rem(x + 1, 4), halves[1]]
            far_w.append(remote(here, here, at_x(3)))
            far_w += [right[1], left[0]]
    for d in (0, 1, 3, 2):
        far[0, d].wait_recv()
        far[1, d].wait_recv()
        here = piece((4 - d) % 4, 2)
        shared.append(remote(here, here, other))
    for copy in far_w:
        copy.wait_recv()
    for copy in shared:
        copy.wait_recv()
    for copy in copies:
        copy.wait_send()
    for copy in swapped:
        pl.when(k == 1)(copy.wait_send)
    pl.when(k == 0)(kept.wait)
    own.wait()


GATHER_COPIES = 6 + 9 + 4 + 16 + 2 + 4


def gather_pages(page_cache, weights):
    rows = page_cache.shape[1]
    anywhere = pl.BlockSpec(memory_space=pl.ANY)
    return pl.pallas_call(
        gather_kernel,
        out_shape=(
            jax.ShapeDtypeStruct((2, 4, 4, 2, rows, HD), jnp.bfloat16),
            jax.ShapeDtypeStruct((4,) + weights.shape, jnp.bfloat16),
        ),
        in_specs=[anywhere, anywhere],
        out_specs=(anywhere, anywhere),
        scratch_shapes=[
            pltpu.SemaphoreType.DMA((6,)),
            pltpu.SemaphoreType.DMA((GATHER_COPIES,)),
            pltpu.SemaphoreType.DMA((GATHER_COPIES,)),
        ],
        compiler_params=pltpu.CompilerParams(collective_id=0, has_side_effects=True),
        name="gather_pages",
    )(page_cache, weights)


LANES = ((0, GROUP * PAGE),)
EXTRA = 16


def attention_kernel(
    slot_ref, parent_ref, count_ref, lost_ref, q_ref, new_ref, kv_ref, out_ref, keys, values, query, top, total,
    score_a, score_b, peak_a, peak_b
):
    scale = math.log2(math.e) / math.sqrt(HD)
    j = pl.program_id(0)
    base = lax.axis_index("ctx") * pl.num_programs(0)
    token = lax.broadcasted_iota(jnp.int32, (16, HD), 0)
    nt = (((1,), (1,)), ((), ()))

    def transposed(block):
        return block.T[: HD + EXTRA]

    def append(state):
        page, filled = state
        count = count_ref[page]
        first = slot_ref[page] * PAGE
        at = pl.ds(pl.multiple_of(first, PAGE), PAGE)
        to = pl.ds(pl.multiple_of(filled, 16), PAGE)
        keys[to, :] = kv_ref[0, at, :]
        values[to, :HD] = kv_ref[1, at, :]
        values[to, HD:] = jnp.ones((PAGE, HD), jnp.bfloat16)
        last = ((count - 1) // 16) * 16
        kept = token + last < count
        at = pl.ds(pl.multiple_of(first + last, 16), 16)
        to = pl.ds(pl.multiple_of(filled + last, 16), 16)
        lead = kv_ref[0, pl.ds(pl.multiple_of(first, PAGE), 16), :].astype(jnp.float32)[:1, :]
        keys[to, :] = jnp.where(kept, kv_ref[0, at, :].astype(jnp.float32), lead).astype(jnp.bfloat16)
        values[to, :HD] = jnp.where(kept, kv_ref[1, at, :].astype(jnp.float32), 0.0).astype(jnp.bfloat16)
        values[to, HD:] = kept.astype(jnp.float32).astype(jnp.bfloat16)
        return parent_ref[page], filled + last + 16

    unused_page, filled = lax.while_loop(
        lambda state: state[0] >= 0, append, (lost_ref[base + j], jnp.int32(0))
    )
    tail = pl.ds(pl.multiple_of(filled, 16), CHUNK)
    lead = keys[:16, :].astype(jnp.float32)[:1, :]
    keys[tail, :] = jnp.broadcast_to(lead, (CHUNK, HD)).astype(jnp.bfloat16)
    values[tail, :] = jnp.zeros((CHUNK, 2 * HD), jnp.bfloat16)
    for h in range(GROUP):
        query[h * PAGE : (h + 1) * PAGE, :] = q_ref[:, h * HD : (h + 1) * HD]

    with_ones = transposed(
        jnp.concatenate([new_ref[1], jnp.ones((PAGE, HD), jnp.bfloat16)], axis=1)
    )
    for start, width in LANES:
        lanes = pl.ds(start, width)
        score = lax.dot_general(
            new_ref[0], query[lanes, :], nt, preferred_element_type=jnp.float32
        )
        k_at = lax.broadcasted_iota(jnp.int32, (PAGE, width), 0)
        q_at = lax.broadcasted_iota(jnp.int32, (PAGE, width), 1) % PAGE
        seen = k_at <= q_at
        score = jnp.where(seen, score, -1e30)
        highest = jnp.max(score, axis=0, keepdims=True)
        weight = jnp.where(seen, jnp.exp2(score * scale - highest * scale), 0.0).astype(jnp.bfloat16)
        top[:, lanes] = jnp.broadcast_to(highest, (8, width))
        total[:, lanes] = jnp.dot(with_ones, weight, preferred_element_type=jnp.float32)

    def look(n, score_ref, peak_ref):
        at = pl.ds(pl.multiple_of(n * CHUNK, CHUNK), CHUNK)
        score = lax.dot_general(keys[at, :], query[...], nt, preferred_element_type=jnp.float32)
        score_ref[...] = score
        peak_ref[...] = jnp.broadcast_to(jnp.max(score, axis=0, keepdims=True), peak_ref.shape)

    def take(n, score_ref, peak_ref):
        at = pl.ds(pl.multiple_of(n * CHUNK, CHUNK), CHUNK)
        before = top[:1, :]
        highest = jnp.maximum(before, peak_ref[:1, :])
        weight = jnp.exp2(score_ref[...] * scale - highest * scale).astype(jnp.bfloat16)
        factor = jnp.exp2((before - highest) * scale)
        top[...] = jnp.broadcast_to(highest, top.shape)
        total[...] = total[...] * factor + jnp.dot(
            transposed(values[at, :]), weight, preferred_element_type=jnp.float32
        )

    def two_chunks(n, unused):
        look(2 * n + 1, score_b, peak_b)
        take(2 * n, score_a, peak_a)
        look(2 * n + 2, score_a, peak_a)
        take(2 * n + 1, score_b, peak_b)
        return unused

    chunks = (filled + CHUNK - 1) // CHUNK
    look(0, score_a, peak_a)
    lax.fori_loop(0, chunks // 2, two_chunks, 0)
    pl.when(chunks % 2 == 1)(lambda: take(chunks - 1, score_a, peak_a))
    for h in range(GROUP):
        lanes = pl.ds(h * PAGE, PAGE)
        out_ref[h * HD : (h + 1) * HD, :] = (total[:HD, lanes] / total[HD : HD + 1, lanes]).astype(
            jnp.bfloat16
        )


def attend(queries, new_kv, kv, page_slot, parent, valid_count, lost_parent):
    rows = kv.shape[1]
    smem = pl.BlockSpec(memory_space=pltpu.SMEM)
    vmem = pl.BlockSpec(memory_space=pltpu.VMEM)
    return pl.pallas_call(
        attention_kernel,
        out_shape=jax.ShapeDtypeStruct(queries.shape[::-1], jnp.bfloat16),
        grid=(queries.shape[0] // PAGE,),
        in_specs=[smem] * 4
        + [
            pl.BlockSpec((PAGE, queries.shape[1]), lambda j: (j, 0)),
            pl.BlockSpec((2, PAGE, HD), lambda j: (0, j, 0)),
            vmem,
        ],
        out_specs=pl.BlockSpec((queries.shape[1], PAGE), lambda j: (0, j)),
        scratch_shapes=[
            pltpu.VMEM((rows + 2 * CHUNK, HD), jnp.bfloat16),
            pltpu.VMEM((rows + CHUNK, 2 * HD), jnp.bfloat16),
            pltpu.VMEM((GROUP * PAGE, HD), jnp.bfloat16),
            pltpu.VMEM((8, GROUP * PAGE), jnp.float32),
            pltpu.VMEM((HD + EXTRA, GROUP * PAGE), jnp.float32),
            pltpu.VMEM((CHUNK, GROUP * PAGE), jnp.float32),
            pltpu.VMEM((CHUNK, GROUP * PAGE), jnp.float32),
            pltpu.VMEM((8, GROUP * PAGE), jnp.float32),
            pltpu.VMEM((8, GROUP * PAGE), jnp.float32),
        ],
        compiler_params=pltpu.CompilerParams(vmem_limit_bytes=VMEM_LIMIT),
        name="attend",
    )(page_slot, parent, valid_count, lost_parent, queries, new_kv, kv)


GROUPS = [
    (((0, 0, 0), (0, 0, 1)), 0),
    (((0, 1, 0), (0, 1, 1)), 0.4),
    (((1, 0, 0), (3, 0, 0)), 1.3),
    (((1, 1, 0), (3, 1, 0)), 1.8),
    (((1, 0, 1), (3, 0, 1)), 2.3),
    (((1, 1, 1), (3, 1, 1)), 2.7),
    (((2, 0, 0), (2, 1, 0)), 2.9),
    (((2, 0, 1), (2, 1, 1)), 3.2),
]
STEPS = 5
EVENTS = [(start - 0.05, parts, None) for parts, start in GROUPS]
EVENTS += [(start + step, parts, step) for parts, start in GROUPS for step in range(STEPS)]
EVENTS.sort(key=lambda event: event[0])
EVEN = ((4, None, 0), (-2, 2, 2), (2, 0, 1))
ODD = ((-3, None, 2), (3, 0, 0), (-1, 2, 3), (1, 1, 1))


def project_kernel(
    own_ref, all_ref, out_ref, att_ref, w_ref, peers, terms, outgoing, incoming, load_sem,
    a_send, a_recv, z_send, z_recv, f_send, f_recv
):
    x, y, k, t = place()
    here = ctx_of(x, y, k)

    def holder(dy, dk):
        return (ctx_of(x, lax.rem(y + dy, 4), k if dk == 0 else 1 - k), t)

    loads = [
        pltpu.make_async_copy(own_ref, att_ref, load_sem.at[0]),
        pltpu.make_async_copy(all_ref, w_ref, load_sem.at[1]),
    ]
    for copy in loads:
        copy.start()
    columns = w_ref.shape[0] // 4
    width = att_ref.shape[1] // 2
    lanes = (pl.ds(0, width), pl.ds(width, width))
    mine = lax.rem(y + k, 2) * 2 + k
    odd = lax.rem(t + lax.div(y, 2) + k, 2)
    barrier = pltpu.get_barrier_semaphore()
    others = [(dy, dk) for dy in range(4) for dk in range(2) if (dy, dk) != (0, 0)]
    for device in [holder(dy, dk) for dy, dk in others] + [(here, lax.rem(t + 1, 8)), (here, lax.rem(t + 7, 8))]:
        pl.semaphore_signal(barrier, inc=1, device_id=device, device_id_type=MESH)
    pl.semaphore_wait(barrier, 9)

    def share(src, dy, dk, side, device):
        copy = pltpu.make_async_remote_copy(
            src,
            peers.at[dy, dk, side],
            a_send.at[dy, dk, side],
            a_recv.at[dy, dk, side],
            device_id=device,
            device_id_type=MESH,
        )
        copy.start()
        return copy

    shared = {}

    def share_near(side):
        mine_here = own_ref.at[:, lanes[side]]
        shared[3, 0, side] = share(mine_here, 3, 0, side, holder(1, 0))
        shared[1, 0, side] = share(mine_here, 1, 0, side, holder(3, 0))

    share_near(0)
    for side in (0, 1):
        shared[0, 1, side] = share(own_ref.at[:, lanes[side]], 0, 1, side, holder(0, 1))

    def need(dy, dk, side):
        if (dy, dk) == (0, 0):
            return
        shared[dy, dk, side].wait_recv()
        if dk == 0:
            if dy == (3 if side == 0 else 1):
                shared[2, 0, side] = share(peers.at[dy, 0, side], 2, 0, side, holder(4 - dy, 0))
            shared[dy, 1, side] = share(peers.at[dy, 0, side], dy, 1, side, holder(0, 1))

    def long_way(part):
        dy, dk, side = part
        return (1 - 2 * k) * (-1 if (dk + side + (dy == 3)) % 2 else 1)

    def hop(part, i, arm, slot):
        dy, dk, side = part
        step = long_way(part) if arm > 0 else -long_way(part)
        return pltpu.make_async_remote_copy(
            outgoing.at[dy, dk, i, side],
            incoming.at[dy, dk, slot, side],
            z_send.at[dy, dk, i, side],
            z_recv.at[dy, dk, slot, side],
            device_id=(here, lax.rem(t + step + 8, 8)),
            device_id_type=MESH,
        )

    def arrived(part, slot):
        dy, dk, side = part
        spot = incoming.at[dy, dk, slot, side]
        pltpu.make_async_copy(spot, spot, z_recv.at[dy, dk, slot, side]).wait()
        return incoming[dy, dk, slot, side].astype(jnp.float32)

    spot = pl.ds(pl.multiple_of(mine * columns, 16), columns)

    def result(part):
        dy, dk, side = part
        return pltpu.make_async_remote_copy(
            outgoing.at[dy, dk, 3, side],
            out_ref.at[spot, lanes[side]],
            f_send.at[dy, dk, side],
            f_recv.at[mine, side],
            device_id=holder(dy, dk),
            device_id_type=MESH,
        )

    def term(part, distance):
        dy, dk, side = part
        target = lax.rem(t + long_way(part) * distance + 8, 8)
        at = pl.ds(pl.multiple_of(lax.div(target, 2) * columns, 32), columns)
        return terms[dy, dk, side, at, :]

    def pass_on(parts, i, table):
        distance, source, slot = table[i]
        for part in parts:
            dy, dk, side = part
            total = term(part, distance)
            if source is not None:
                total = total + arrived(part, source)
            outgoing[dy, dk, i, side] = total.astype(jnp.bfloat16)
            hop(part, i, distance, slot).start()

    def finish(parts):
        for part in parts:
            dy, dk, side = part
            total = term(part, 0) + arrived(part, 3) + arrived(part, 1)
            if (dy, dk) == (0, 0):
                out_ref[spot, lanes[side]] = total.astype(jnp.bfloat16)
            else:
                outgoing[dy, dk, 3, side] = total.astype(jnp.bfloat16)
                result(part).start()

    def multiply(parts):
        for part in parts:
            need(*part)
        if parts[0][:2] == (0, 0):
            rows = att_ref[...]
        else:
            rows = jnp.concatenate([peers[part] for part in parts], axis=1)
        products = jnp.dot(w_ref[...], rows, preferred_element_type=jnp.float32)
        for n, (dy, dk, side) in enumerate(parts):
            terms[dy, dk, side] = products[:, n * width : (n + 1) * width]

    for copy in loads:
        copy.wait()
    for unused_time, parts, i in EVENTS:
        if i is None:
            if parts[0][0] == 1 and (1, 0, 1) not in shared:
                share_near(1)
            multiply(parts)
            continue
        if i < 4:
            pl.when(odd == 1)(lambda parts=parts, i=i: pass_on(parts, i, ODD))
        if i < 3:
            pl.when(odd == 0)(lambda parts=parts, i=i: pass_on(parts, i, EVEN))
        if i == 4:
            pl.when(odd == 0)(lambda parts=parts: finish(parts))

    for n in range(4):

        @pl.when((odd == 1) | (mine != n))
        def _(n=n):
            for side in (0, 1):
                landed = out_ref.at[pl.ds(n * columns, columns), lanes[side]]
                pltpu.make_async_copy(landed, landed, f_recv.at[n, side]).wait()

    for copy in shared.values():
        copy.wait_send()

    def drain(part, table):
        for i, (distance, source, slot) in enumerate(table):
            hop(part, i, distance, slot).wait_send()

    for parts, unused_start in GROUPS:
        for part in parts:
            pl.when(odd == 1)(lambda part=part: drain(part, ODD))

            @pl.when(odd == 0)
            def _(part=part):
                drain(part, EVEN)
                if part[:2] != (0, 0):
                    result(part).wait_send()


def project(attended, weights):
    depth, rows = attended.shape
    columns = weights.shape[0] // 4
    vmem = pl.BlockSpec(memory_space=pltpu.VMEM)
    return pl.pallas_call(
        project_kernel,
        out_shape=jax.ShapeDtypeStruct((4 * columns, rows), jnp.bfloat16),
        in_specs=[pl.BlockSpec(memory_space=pl.ANY)] * 2,
        out_specs=vmem,
        scratch_shapes=[
            pltpu.VMEM((depth, rows), jnp.bfloat16),
            pltpu.VMEM(weights.shape, jnp.bfloat16),
            pltpu.VMEM((4, 2, 2, depth, rows // 2), jnp.bfloat16),
            pltpu.VMEM((4, 2, 2, 4 * columns, rows // 2), jnp.float32),
            pltpu.VMEM((4, 2, 4, 2, columns, rows // 2), jnp.bfloat16),
            pltpu.VMEM((4, 2, 4, 2, columns, rows // 2), jnp.bfloat16),
            pltpu.SemaphoreType.DMA((2,)),
            pltpu.SemaphoreType.DMA((4, 2, 2)),
            pltpu.SemaphoreType.DMA((4, 2, 2)),
            pltpu.SemaphoreType.DMA((4, 2, 4, 2)),
            pltpu.SemaphoreType.DMA((4, 2, 4, 2)),
            pltpu.SemaphoreType.DMA((4, 2, 2)),
            pltpu.SemaphoreType.DMA((4, 2)),
        ],
        compiler_params=pltpu.CompilerParams(
            collective_id=1, has_side_effects=True, vmem_limit_bytes=VMEM_LIMIT
        ),
        name="project",
    )(attended, weights)


def per_device(
    queries, new_kv, page_cache, out_weight, page_slot, parent, valid_count, lost_parent
):
    kv, weights = gather_pages(page_cache, out_weight.T)
    kv = kv.reshape(2, -1, HD)
    attended = attend(queries, new_kv, kv, page_slot, parent, valid_count, lost_parent)
    return project(attended, weights.reshape(-1, weights.shape[2])).T


def solution(mesh):
    return jax.shard_map(
        per_device,
        mesh=mesh,
        in_specs=(
            P("ctx", "tp"),
            P(None, "ctx", "tp"),
            P(None, "ctx", "tp"),
            P("tp", "ctx"),
            P(),
            P(),
            P(),
            P(),
        ),
        out_specs=P("ctx", "tp"),
        check_vma=False,
    )
```
